256 devices in a mesh: row: 8 (over x, core), col: 32 (over z, y).
Axes of the slice: x: 4, y: 4, z: 8, core: 2. Of those that a mesh axis runs over, the one named last changes fastest.
Arguments:
- points: float32 [65536, 32], P(('row', 'col')), may hold values from -6 to 6
- inv_length: float32 [32], replicated, may hold values from 0.1 to 0.3
- solution: float32 [65536, 8], P(('row', 'col')), may hold values from -6 to 6
- residual: float32 [65536, 8], P(('row', 'col')), may hold values from -6 to 6
- direction: float32 [65536, 8], P(('row', 'col')), may hold values from -6 to 6
Outputs:
- new_solution: float32 [65536, 8], P(('row', 'col'))
- new_residual: float32 [65536, 8], P(('row', 'col'))
- new_direction: float32 [65536, 8], P(('row', 'col'))
The draws below stay inside these ranges and needn't reach their ends.
All inputs are finite; a program needn't handle non-finite values.
Results may differ from the reference program's by a relative error of at most 0.00011.
Values sent between devices are 32-bit elements; how exact they have to be, the bound alone decides.
A program may use at most 192 MiB of HBM per device.

```python
import math
import jax
import jax.numpy as jnp
from jax import lax

DIM = 32
RHS = 8
NPTS = 65536


def steps_of(own_key, extent, split, least, largest):
    loudness, own = 1.0, jax.random.fold_in(own_key, 6)
    for position, shards_of in split:
        steps = jnp.exp(jax.random.uniform(jax.random.fold_in(own, position), (shards_of,), jnp.float32, least / len(split), largest / len(split)))
        loudness = loudness * jnp.repeat(steps, extent[position] // shards_of).reshape([-1 if axis == position else 1 for axis in range(len(extent))])
    return loudness


def scatter_about(stream_key, dims, scale, limit, split=(), kind=jnp.bfloat16):
    factor_of = steps_of(stream_key, dims, split, -0.22, 0.18) if split else 1.0
    entries = jax.random.normal(stream_key, dims, jnp.float32) * scale * factor_of
    return jnp.minimum(jnp.maximum(entries, -limit), limit).astype(kind)


def setup_inputs(seed: int = 0) -> dict:
    splits = jax.random.split(jax.random.key(seed), 6)
    points = scatter_about(splits[0], (NPTS, DIM), 1.0, 6.0, ((0, 256),), jnp.float32)
    inv_length = jnp.clip(jnp.exp(jax.random.uniform(splits[1], (DIM,), jnp.float32, math.log(0.1), math.log(0.3))), 0.1, 0.3)
    solution = scatter_about(splits[2], (NPTS, RHS), 1.0, 6.0, ((0, 256),), jnp.float32)
    residual = scatter_about(splits[3], (NPTS, RHS), 1.0, 6.0, ((0, 256),), jnp.float32)
    direction = scatter_about(splits[4], (NPTS, RHS), 1.0, 6.0, ((0, 256),), jnp.float32)
    return {"points": points, "inv_length": inv_length, "solution": solution, "residual": residual, "direction": direction}


root_five = math.sqrt(5.0)
noise_level = 0.1

def kernel_product(row_s, row_q, col_s, col_q, col_v):
    cross = jnp.dot(row_s, col_s.T, precision=lax.Precision.HIGHEST, preferred_element_type=jnp.float32)
    dist_sq = jnp.maximum(row_q[:, None] + col_q[None, :] - 2.0 * cross, 0.0)
    scaled_r = root_five * jnp.sqrt(dist_sq)
    kernel = (1.0 + scaled_r + scaled_r * scaled_r / 3.0) * jnp.exp(-scaled_r)
    return jnp.dot(kernel, col_v, precision=lax.Precision.HIGHEST, preferred_element_type=jnp.float32)

def reference(points, inv_length, solution, residual, direction):
    scaled = points * inv_length
    squares = lax.optimization_barrier(jnp.sum(scaled * scaled, axis=1))
    height = math.gcd(NPTS, 1024)
    row_blocks = scaled.reshape(NPTS // height, height, DIM)
    row_norms = squares.reshape(NPTS // height, height)

    def one_block(operands):
        return kernel_product(operands[0], operands[1], scaled, squares, direction)
    image = lax.map(one_block, (row_blocks, row_norms)).reshape(NPTS, RHS)
    image = image + noise_level * direction
    norm_old = lax.optimization_barrier(jnp.sum(residual * residual, axis=0))
    curvature = lax.optimization_barrier(jnp.sum(direction * image, axis=0))
    step_size = norm_old / curvature
    new_solution = solution + step_size * direction
    new_residual = residual - step_size * image
    norm_new = lax.optimization_barrier(jnp.sum(new_residual * new_residual, axis=0))
    new_direction = new_residual + norm_new / norm_old * direction
    return (new_solution, new_residual, new_direction)
```

```python
import functools
import math

import jax
import jax.numpy as jnp
from jax import lax
from jax.experimental import pallas as pl
from jax.experimental.pallas import tpu as pltpu
from jax.sharding import PartitionSpec as P

F = jnp.float32
H = jnp.bfloat16
MESH = pl.DeviceIdType.MESH
noise_level = 0.1
LOG2E = 1.0 / math.log(2.0)
SCALE = math.sqrt(5.0) * LOG2E
C1 = 3.0 * LOG2E
C0 = 3.0 * LOG2E * LOG2E
GAIN = 1.0 / C0
DIM = 32
RHS = 8
PACK = DIM + RHS
DEPTH = 256


def offsets(nz, ny):
    def hop(d, n):
        return min(d, n - d)

    whole, half, load = [], [], {}
    every = sorted(
        ((dz, dy) for dz in range(nz) for dy in range(ny)),
        key=lambda o: (hop(o[0], nz) + hop(o[1], ny), o),
    )

    def charge(o):
        dz, dy = o
        out = {}
        if dz and 2 * dz != nz:
            out["z+" if 2 * dz < nz else "z-"] = hop(dz, nz)
        if dy and 2 * dy != ny:
            out["y+" if 2 * dy < ny else "y-"] = hop(dy, ny)
        return out

    for o in every:
        back = ((-o[0]) % nz, (-o[1]) % ny)
        if o == (0, 0):
            continue
        if o == back:
            half.append(o)
            continue
        if o in whole or back in whole:
            continue

        def cost(cand):
            trial = dict(load)
            for key, hops in charge(cand).items():
                trial[key] = trial.get(key, 0) + hops
            return sum(v * v for v in trial.values())

        pick = min((o, back), key=cost)
        for key, hops in charge(pick).items():
            load[key] = load.get(key, 0) + hops
        whole.append(pick)
    return whole, half


def pieces(x):
    first = x.astype(H).astype(F)
    rest = x - first
    second = rest.astype(H).astype(F)
    third = (rest - second).astype(H).astype(F)
    return first, second, third


def norms(scaled):
    return jnp.sum(scaled * scaled, axis=0, keepdims=True)


def stack_left(block, width):
    scaled = block[:DIM, :]
    h, m, l = pieces(scaled)
    qh, qm, ql = pieces(norms(scaled))
    one = jnp.ones((1, width), F)
    zero = jnp.zeros((DEPTH - 6 * DIM - 8, width), F)
    tail = jnp.concatenate([qh, qm, ql, one, one, one, zero[:2]], axis=0)
    return jnp.concatenate([h, h, m, m, h, l, tail, zero], axis=0)


def stack_right(block, width):
    scaled = block[:DIM, :]
    h, m, l = pieces(scaled)
    h, m, l = -2.0 * h, -2.0 * m, -2.0 * l
    qh, qm, ql = pieces(norms(scaled))
    one = jnp.ones((1, width), F)
    zero = jnp.zeros((DEPTH - 6 * DIM - 8, width), F)
    tail = jnp.concatenate([one, one, one, qh, qm, ql, zero[:2]], axis=0)
    return jnp.concatenate([h, m, h, m, l, h, tail, zero], axis=0)


def two_pieces(v):
    first = v.astype(H).astype(F)
    return jnp.concatenate([first, v - first], axis=0)


def matern(x):
    x = jnp.maximum(x, 1e-30)
    t = x * lax.rsqrt(x)
    return (t * (t + C1) + C0) * jnp.exp2(-t)


def kernel(
    plan,
    pts_ref, inv_ref, sol_ref, res_ref, dir_ref,
    new_sol_ref, new_res_ref, new_dir_ref,
    pack, gather_a, gather_b, rows_b, vals_b, sums_b,
    send_a, send_b, back_a, back_b, red_row, red_z, red_y,
    ga_send, ga_recv, gb_send, gb_recv, ra_send, ra_recv, rb_send, rb_recv,
    rr_send, rr_recv, rz_send, rz_recv, ry_send, ry_recv,
):
    nr, nz, ny, whole, half = plan
    width = pts_ref.shape[1]
    r = lax.axis_index("row")
    c = lax.axis_index("col")
    z, y = c // ny, c % ny
    every = whole + half

    def shift(dz, dy):
        return (r, lax.rem(z + dz, nz) * ny + lax.rem(y + dy, ny))

    def row_shift(o):
        return (lax.rem(r + o, nr), c)

    def opposite(o):
        return ((nz - o[0]) % nz, (ny - o[1]) % ny)

    def remote(src, dst, send_sem, recv_sem, device):
        return pltpu.make_async_remote_copy(
            src_ref=src, dst_ref=dst, send_sem=send_sem, recv_sem=recv_sem,
            device_id=device, device_id_type=MESH,
        )

    barrier = pltpu.get_barrier_semaphore()
    for o in every:
        pl.semaphore_signal(barrier, inc=1, device_id=shift(*opposite(o)), device_id_type=MESH)
    for o in range(1, nr):
        pl.semaphore_signal(barrier, inc=1, device_id=row_shift(o), device_id_type=MESH)

    lengths = jnp.transpose(jnp.broadcast_to(inv_ref[...], (DIM, DIM)))[:, :1]
    pack[0:DIM, :] = pts_ref[...] * lengths * SCALE
    pack[DIM:PACK, :] = dir_ref[...]
    pl.semaphore_wait(barrier, len(every) + nr - 1)

    sends = []
    for o in range(1, nr):
        sends.append(remote(pack, gather_b.at[o], gb_send.at[o], gb_recv.at[o], row_shift(nr - o)))
    for i, o in enumerate(every):
        sends.append(remote(pack, gather_a.at[i], ga_send.at[i], ga_recv.at[i], shift(*o)))
    for copy in sends:
        copy.start()

    def prepare_b(o, block):
        at = pl.ds(pl.multiple_of(o * width, width), width)
        rows_b[at, :] = jnp.transpose(stack_right(block, width)).astype(H)
        vals_b[:, at] = two_pieces(block[DIM:PACK, :]).astype(H)

    prepare_b(0, pack[...])

    def arrive_b(o, carry):
        remote(pack, gather_b.at[o], gb_send.at[o], gb_recv.at[o], row_shift(1)).wait_recv()
        prepare_b(o, gather_b[o])
        return carry

    lax.fori_loop(1, nr, arrive_b, 0)
    sums_b[...] = jnp.zeros_like(sums_b)

    def prepare_a(block):
        left = stack_left(block, width).astype(H)
        vals = jnp.transpose(two_pieces(block[DIM:PACK, :])).astype(H)
        return left, jnp.concatenate([vals, vals], axis=0)

    def strip(left, rows):
        k = matern(jnp.dot(rows, left, preferred_element_type=F))
        high = k.astype(H)
        low = (k - high.astype(F)).astype(H)
        return high, low

    def down(values, high, low):
        out = jnp.dot(
            jnp.concatenate([values, values], axis=1),
            jnp.concatenate([high, low], axis=0),
            preferred_element_type=F,
        )
        return out[:RHS] + out[RHS:]

    def across(high, low, vals):
        return jnp.dot(jnp.concatenate([high, low], axis=1), vals, preferred_element_type=F)

    span = (nr // 2 + 1) * width
    left, vals = prepare_a(pack[...])
    high, low = strip(left, rows_b[:span, :])
    own = vals_b[:, :span]
    lane = lax.broadcasted_iota(jnp.int32, (1, span), 1)
    own = jnp.where(lane >= span - width, own.astype(F) * 0.5, own.astype(F)).astype(H)
    image = down(own, high, low)
    part = across(high[width:], low[width:], vals)
    line = lax.broadcasted_iota(jnp.int32, (span - width, 1), 0)
    part = jnp.where(line >= span - 2 * width, part * 0.5, part)
    sums_b[width:span, :] += part

    def table(i, entries):
        out = jnp.int32(entries[0])
        for n in range(1, len(entries)):
            out = jnp.where(i == n, jnp.int32(entries[n]), out)
        return out

    def give_back(i, value, entries, base):
        send_a[i] = value
        back = [opposite(o) for o in entries]
        dz = table(i - base, [o[0] for o in back])
        dy = table(i - base, [o[1] for o in back])
        remote(send_a.at[i], back_a.at[i], ra_send.at[i], ra_recv.at[i], shift(dz, dy)).start()

    def whole_strip(i, carry):
        remote(pack, gather_a.at[i], ga_send.at[i], ga_recv.at[i], row_shift(1)).wait_recv()
        left, vals = prepare_a(gather_a[i])
        high, low = strip(left, rows_b[...])
        give_back(i, down(vals_b[...], high, low), whole, 0)
        sums_b[...] += across(high, low, vals)
        return carry

    lax.fori_loop(0, len(whole), whole_strip, 0)

    halves = []
    for dz, dy in half:
        halves.append(2 * z // nz if dz else 2 * y // ny)

    def half_strip(i, carry):
        n = i - len(whole)
        remote(pack, gather_a.at[i], ga_send.at[i], ga_recv.at[i], row_shift(1)).wait_recv()
        left, vals = prepare_a(gather_a[i])
        side = halves[0]
        for k in range(1, len(halves)):
            side = jnp.where(n == k, halves[k], side)
        at = pl.ds(pl.multiple_of((1 - side) * width, width), nr // 2 * width)
        high, low = strip(left, rows_b[at, :])
        give_back(i, down(vals_b[:, at], high, low), half, len(whole))
        sums_b[at, :] += across(high, low, vals)
        return carry

    lax.fori_loop(len(whole), len(every), half_strip, 0)

    for o in range(nr):
        total = sums_b[o * width:(o + 1) * width, :]
        flipped = jnp.transpose(total)
        flipped = flipped[:RHS] + flipped[RHS:]
        if o == 0:
            image = image + flipped
        else:
            send_b[o] = flipped
            copy = remote(send_b.at[o], back_b.at[o], rb_send.at[o], rb_recv.at[o], row_shift(o))
            copy.start()
            sends.append(copy)

    for i in range(len(every)):
        copy = remote(send_a.at[i], back_a.at[i], ra_send.at[i], ra_recv.at[i], row_shift(1))
        copy.wait_recv()
        image = image + back_a[i]
    for o in range(1, nr):
        remote(send_b.at[o], back_b.at[o], rb_send.at[o], rb_recv.at[o], row_shift(1)).wait_recv()
        image = image + back_b[o]

    direction = dir_ref[...]
    residual = res_ref[...]
    image = GAIN * image + noise_level * direction

    def reduce_all(turn, value):
        for size, buf, ssem, rsem, mine, peer in (
            (nr, red_row, rr_send, rr_recv, r, lambda e: (lax.rem(r + e, nr), c)),
            (nz, red_z, rz_send, rz_recv, z, lambda e: shift(e, 0)),
            (ny, red_y, ry_send, ry_recv, y, lambda e: shift(0, e)),
        ):
            buf[turn, mine] = value
            for e in range(1, size):
                copy = remote(buf.at[turn, mine], buf.at[turn, mine], ssem.at[turn, e], rsem.at[turn, mine], peer(e))
                copy.start()
                sends.append(copy)
            for e in range(1, size):
                other = lax.rem(mine + e, size)
                remote(buf.at[turn, other], buf.at[turn, other], ssem.at[turn, e], rsem.at[turn, other], peer(e)).wait_recv()
            value = buf[turn, 0]
            for e in range(1, size):
                value = value + buf[turn, e]
        return value

    lane = lax.broadcasted_iota(jnp.int32, (RHS, 128), 1)
    old = jnp.sum(residual * residual, axis=1, keepdims=True)
    curve = jnp.sum(direction * image, axis=1, keepdims=True)
    both = reduce_all(0, jnp.where(lane == 0, old, curve))
    old, curve = both[:, 0:1], both[:, 1:2]
    step = old / curve
    new_sol_ref[...] = sol_ref[...] + step * direction
    fresh = residual - step * image
    new_res_ref[...] = fresh
    new = reduce_all(1, jnp.broadcast_to(jnp.sum(fresh * fresh, axis=1, keepdims=True), (RHS, 128)))[:, 0:1]
    new_dir_ref[...] = fresh + new / old * direction

    for copy in sends:
        copy.wait_send()

    def sent(i, carry):
        remote(send_a.at[i], back_a.at[i], ra_send.at[i], ra_recv.at[i], row_shift(1)).wait_send()
        return carry

    lax.fori_loop(0, len(every), sent, 0)


def solution(mesh):
    nr, nc = mesh.shape["row"], mesh.shape["col"]
    ny = 4 if nc == 32 else 2
    nz = nc // ny
    whole, half = offsets(nz, ny)
    na = len(whole) + len(half)

    def local(points, inv_length, solution_, residual, direction):
        width = points.shape[0]
        vmem = pl.BlockSpec(memory_space=pltpu.VMEM)
        dma = pltpu.SemaphoreType.DMA
        out = jax.ShapeDtypeStruct((RHS, width), F)
        flat = pl.pallas_call(
            functools.partial(kernel, (nr, nz, ny, whole, half)),
            out_shape=(out, out, out),
            in_specs=[vmem] * 5,
            out_specs=(vmem, vmem, vmem),
            scratch_shapes=[
                pltpu.VMEM((PACK, width), F),
                pltpu.VMEM((na, PACK, width), F),
                pltpu.VMEM((nr, PACK, width), F),
                pltpu.VMEM((nr * width, DEPTH), H),
                pltpu.VMEM((2 * RHS, nr * width), H),
                pltpu.VMEM((nr * width, 2 * RHS), F),
                pltpu.VMEM((na, RHS, width), F),
                pltpu.VMEM((nr, RHS, width), F),
                pltpu.VMEM((na, RHS, width), F),
                pltpu.VMEM((nr, RHS, width), F),
                pltpu.VMEM((2, nr, RHS, 128), F),
                pltpu.VMEM((2, nz, RHS, 128), F),
                pltpu.VMEM((2, ny, RHS, 128), F),
                dma((na,)), dma((na,)), dma((nr,)), dma((nr,)),
                dma((na,)), dma((na,)), dma((nr,)), dma((nr,)),
                dma((2, nr)), dma((2, nr)), dma((2, nz)), dma((2, nz)), dma((2, ny)), dma((2, ny)),
            ],
            compiler_params=pltpu.CompilerParams(
                collective_id=0, has_side_effects=True, vmem_limit_bytes=48 * 2**20
            ),
            cost_estimate=pl.CostEstimate(flops=2 * 10**10, bytes_accessed=10**6, transcendentals=2 * 10**7),
        )(points.T, inv_length.reshape(1, DIM), solution_.T, residual.T, direction.T)
        return tuple(x.T for x in flat)

    placed = (
        P(("row", "col"), None),
        P(),
        P(("row", "col"), None),
        P(("row", "col"), None),
        P(("row", "col"), None),
    )
    return jax.shard_map(
        local,
        mesh=mesh,
        in_specs=placed,
        out_specs=(P(("row", "col"), None),) * 3,
        check_vma=False,
    )
```

```python
import functools
import math

import jax
import jax.numpy as jnp
from jax import lax
from jax.experimental import pallas as pl
from jax.experimental.pallas import tpu as pltpu
from jax.sharding import PartitionSpec as P

F = jnp.float32
H = jnp.bfloat16
MESH = pl.DeviceIdType.MESH
noise_level = 0.1
LOG2E = 1.0 / math.log(2.0)
SCALE = math.sqrt(5.0) * LOG2E
C1 = 3.0 * LOG2E
C0 = 3.0 * LOG2E * LOG2E
GAIN = 1.0 / C0
DIM = 32
RHS = 8
PACK = DIM + RHS
DEPTH = 256


def offsets(nz, ny):
    def hop(d, n):
        return min(d, n - d)

    whole, half, load = [], [], {}
    every = sorted(
        ((dz, dy) for dz in range(nz) for dy in range(ny)),
        key=lambda o: (hop(o[0], nz) + hop(o[1], ny), o),
    )

    def charge(o):
        dz, dy = o
        out = {}
        if dz and 2 * dz != nz:
            out["z+" if 2 * dz < nz else "z-"] = hop(dz, nz)
        if dy and 2 * dy != ny:
            out["y+" if 2 * dy < ny else "y-"] = hop(dy, ny)
        return out

    for o in every:
        back = ((-o[0]) % nz, (-o[1]) % ny)
        if o == (0, 0):
            continue
        if o == back:
            half.append(o)
            continue
        if o in whole or back in whole:
            continue

        def cost(cand):
            trial = dict(load)
            for key, hops in charge(cand).items():
                trial[key] = trial.get(key, 0) + hops
            return sum(v * v for v in trial.values())

        pick = min((o, back), key=cost)
        for key, hops in charge(pick).items():
            load[key] = load.get(key, 0) + hops
        whole.append(pick)
    return whole, half


def pieces(x):
    first = x.astype(H).astype(F)
    rest = x - first
    second = rest.astype(H).astype(F)
    third = (rest - second).astype(H).astype(F)
    return first, second, third


def norms(scaled):
    return jnp.sum(scaled * scaled, axis=0, keepdims=True)


def stack_left(block, width):
    scaled = block[:DIM, :]
    h, m, l = pieces(scaled)
    qh, qm, ql = pieces(norms(scaled))
    one = jnp.ones((1, width), F)
    zero = jnp.zeros((DEPTH - 6 * DIM - 8, width), F)
    tail = jnp.concatenate([qh, qm, ql, one, one, one, zero[:2]], axis=0)
    return jnp.concatenate([h, h, m, m, h, l, tail, zero], axis=0)


def stack_right(block, width):
    scaled = block[:DIM, :]
    h, m, l = pieces(scaled)
    h, m, l = -2.0 * h, -2.0 * m, -2.0 * l
    qh, qm, ql = pieces(norms(scaled))
    one = jnp.ones((1, width), F)
    zero = jnp.zeros((DEPTH - 6 * DIM - 8, width), F)
    tail = jnp.concatenate([one, one, one, qh, qm, ql, zero[:2]], axis=0)
    return jnp.concatenate([h, m, h, m, l, h, tail, zero], axis=0)


def two_pieces(v):
    first = v.astype(H).astype(F)
    return jnp.concatenate([first, v - first], axis=0)


def matern(x):
    x = jnp.maximum(x, 1e-30)
    t = x * lax.rsqrt(x)
    return (t * (t + C1) + C0) * jnp.exp2(-t)


def two_sum(a, b):
    s = a + b
    t = s - a
    return s, (a - (s - t)) + (b - t)


def split(a):
    c = a * 4097.0
    high = c - (c - a)
    return high, a - high


def two_product(a, b):
    p = a * b
    ah, al = split(a)
    bh, bl = split(b)
    return p, ((ah * bh - p) + ah * bl + al * bh) + al * bl


def add_pairs(a, b):
    s, e = two_sum(a[0], b[0])
    return s, e + (a[1] + b[1])


def settle(a):
    return two_sum(a[0], a[1])


def scale_pair(a, f):
    p, e = two_product(a[0], f)
    return settle((p, e + a[1] * f))


def tree(items, join):
    while len(items) > 1:
        items = [join(*items[i:i + 2]) if i + 1 < len(items) else items[i] for i in range(0, len(items), 2)]
    return items[0]


def dot_pair(a, b):
    p, e = two_product(a, b)
    n = a.shape[1] // 128
    pair = tree([(p[:, i * 128:(i + 1) * 128], e[:, i * 128:(i + 1) * 128]) for i in range(n)], add_pairs)
    for shift in (64, 32, 16, 8, 4, 2, 1):
        pair = add_pairs(pair, tuple(pltpu.roll(x, shift, 1) for x in pair))
    return pair


def kernel(
    plan,
    pts_hbm, inv_hbm, sol_hbm, res_hbm, dir_hbm,
    new_sol_ref, new_res_ref, new_dir_ref,
    pts_ref, inv_ref, sol_ref, res_ref, dir_ref,
    pack, gather_a, gather_b, rows_b, vals_b, sums_b,
    send_a, send_b, back_a, back_b, red_row, red_col,
    in_sem, ga_send, ga_recv, gb_send, gb_recv, ra_send, ra_recv, rb_send, rb_recv,
    rr_send, rr_recv, rc_send, rc_recv,
):
    nr, nz, ny, whole, half = plan
    nx = nr // 2
    width = pts_ref.shape[1]
    r = lax.axis_index("row")
    c = lax.axis_index("col")
    z, y = c // ny, c % ny
    x, core = r // 2, r % 2
    every = whole + half

    def shift(dz, dy):
        return (r, lax.rem(z + dz, nz) * ny + lax.rem(y + dy, ny))

    def row_shift(o, sign=1):
        dx = (o // 2) if sign > 0 else (nx - o // 2) % nx
        return (lax.rem(x + dx, nx) * 2 + lax.rem(core + o % 2, 2), c)

    def opposite(o):
        return ((nz - o[0]) % nz, (ny - o[1]) % ny)

    def remote(src, dst, send_sem, recv_sem, device):
        return pltpu.make_async_remote_copy(
            src_ref=src, dst_ref=dst, send_sem=send_sem, recv_sem=recv_sem,
            device_id=device, device_id_type=MESH,
        )

    barrier = pltpu.get_barrier_semaphore()
    for o in every:
        pl.semaphore_signal(barrier, inc=1, device_id=shift(*opposite(o)), device_id_type=MESH)
    for o in range(1, nr):
        pl.semaphore_signal(barrier, inc=1, device_id=row_shift(o), device_id_type=MESH)

    loads = [
        pltpu.make_async_copy(src, dst, in_sem.at[i])
        for i, (src, dst) in enumerate((
            (pts_hbm, pts_ref), (dir_hbm, dir_ref), (inv_hbm, inv_ref), (res_hbm, res_ref), (sol_hbm, sol_ref),
        ))
    ]
    for copy in loads:
        copy.start()
    sums_b[...] = jnp.zeros_like(sums_b)
    for copy in loads:
        copy.wait()

    lengths = jnp.transpose(jnp.broadcast_to(inv_ref[...], (DIM, DIM)))[:, :1]
    pack[0:DIM, :] = pts_ref[...] * lengths * SCALE
    pack[DIM:PACK, :] = dir_ref[...]
    pl.semaphore_wait(barrier, len(every) + nr - 1)

    sends = []
    for o in range(1, nr):
        sends.append(remote(pack, gather_b.at[o], gb_send.at[o], gb_recv.at[o], row_shift(o, -1)))
    for i, o in enumerate(every):
        sends.append(remote(pack, gather_a.at[i], ga_send.at[i], ga_recv.at[i], shift(*o)))
    for copy in sends:
        copy.start()

    def prepare_b(o, block):
        at = pl.ds(pl.multiple_of(o * width, width), width)
        rows_b[at, :] = jnp.transpose(stack_right(block, width)).astype(H)
        vals_b[:, at] = two_pieces(block[DIM:PACK, :]).astype(H)

    prepare_b(0, pack[...])

    def arrive_b(o, carry):
        remote(pack, gather_b.at[o], gb_send.at[o], gb_recv.at[o], row_shift(1)).wait_recv()
        prepare_b(o, gather_b[o])
        return carry

    lax.fori_loop(1, nr, arrive_b, 0)

    def prepare_a(block):
        left = stack_left(block, width).astype(H)
        vals = jnp.transpose(two_pieces(block[DIM:PACK, :])).astype(H)
        return left, jnp.concatenate([vals, vals], axis=0)

    def strip(left, rows):
        k = matern(jnp.dot(rows, left, preferred_element_type=F))
        high = k.astype(H)
        low = (k - high.astype(F)).astype(H)
        return high, low

    def down(values, high, low):
        out = jnp.dot(
            jnp.concatenate([values, values], axis=1),
            jnp.concatenate([high, low], axis=0),
            preferred_element_type=F,
        )
        return out[:RHS] + out[RHS:]

    def across(high, low, vals):
        return jnp.dot(jnp.concatenate([high, low], axis=1), vals, preferred_element_type=F)

    def table(i, entries):
        out = jnp.int32(entries[0])
        for n in range(1, len(entries)):
            out = jnp.where(i == n, jnp.int32(entries[n]), out)
        return out

    def give_back(i, value, entries, base):
        send_a[i] = value
        back = [opposite(o) for o in entries]
        dz = table(i - base, [o[0] for o in back])
        dy = table(i - base, [o[1] for o in back])
        remote(send_a.at[i], back_a.at[i], ra_send.at[i], ra_recv.at[i], shift(dz, dy)).start()

    def whole_strip(i, carry):
        remote(pack, gather_a.at[i], ga_send.at[i], ga_recv.at[i], row_shift(1)).wait_recv()
        left, vals = prepare_a(gather_a[i])
        high, low = strip(left, rows_b[...])
        give_back(i, down(vals_b[...], high, low), whole, 0)
        sums_b[...] += across(high, low, vals)
        return carry

    lax.fori_loop(0, len(whole), whole_strip, 0)

    halves = []
    for dz, dy in half:
        halves.append(2 * z // nz if dz else 2 * y // ny)

    def half_strip(i, carry):
        n = i - len(whole)
        remote(pack, gather_a.at[i], ga_send.at[i], ga_recv.at[i], row_shift(1)).wait_recv()
        left, vals = prepare_a(gather_a[i])
        side = halves[0]
        for k in range(1, len(halves)):
            side = jnp.where(n == k, halves[k], side)
        at = pl.ds(pl.multiple_of((1 - side) * 2 * width, 2 * width), nr // 2 * width)
        high, low = strip(left, rows_b[at, :])
        give_back(i, down(vals_b[:, at], high, low), half, len(whole))
        sums_b[at, :] += across(high, low, vals)
        return carry

    lax.fori_loop(len(whole), len(every), half_strip, 0)

    for o in range(1, nr):
        flipped = jnp.transpose(sums_b[o * width:(o + 1) * width, :])
        send_b[o] = flipped[:RHS] + flipped[RHS:]
        copy = remote(send_b.at[o], back_b.at[o], rb_send.at[o], rb_recv.at[o], row_shift(o))
        copy.start()
        sends.append(copy)
    flipped = jnp.transpose(sums_b[0:width, :])
    image = flipped[:RHS] + flipped[RHS:]

    left, _ = prepare_a(pack[...])
    high, low = strip(left, rows_b[...])
    image = image + down(vals_b[...], high, low)

    for i in range(len(every)):
        copy = remote(send_a.at[i], back_a.at[i], ra_send.at[i], ra_recv.at[i], row_shift(1))
        copy.wait_recv()
        image = image + back_a[i]
    for o in range(1, nr):
        remote(send_b.at[o], back_b.at[o], rb_send.at[o], rb_recv.at[o], row_shift(1)).wait_recv()
        image = image + back_b[o]

    direction = dir_ref[...]
    residual = res_ref[...]
    image = GAIN * image + noise_level * direction

    lane = lax.broadcasted_iota(jnp.int32, (RHS, 128), 1)
    pairs = [dot_pair(residual, residual), dot_pair(direction, image), dot_pair(residual, image), dot_pair(image, image)]
    mixed = jnp.zeros((RHS, 128), F)
    for q, pair in enumerate(pairs):
        mixed = jnp.where(lane == q, pair[0], jnp.where(lane == q + 4, pair[1], mixed))
    value = jnp.sum(pltpu.roll(mixed, 0, 1, stride=8, stride_axis=0), axis=0, keepdims=True)
    first = lax.broadcasted_iota(jnp.int32, (1, 128), 1) % 8 < 4

    for size, buf, ssem, rsem, mine, peer in (
        (nr, red_row, rr_send, rr_recv, r, lambda e: (lax.rem(r + e, nr), c)),
        (nz * ny, red_col, rc_send, rc_recv, c, lambda e: (r, lax.rem(c + e, nz * ny))),
    ):
        buf[mine] = value
        for e in range(1, size):
            copy = remote(buf.at[mine], buf.at[mine], ssem.at[e], rsem.at[mine], peer(e))
            copy.start()
            sends.append(copy)
        for e in range(1, size):
            other = lax.rem(mine + e, size)
            remote(buf.at[other], buf.at[other], ssem.at[e], rsem.at[other], peer(e)).wait_recv()
        total, error = tree([(buf[e], jnp.zeros((1, 128), F)) for e in range(size)], add_pairs)
        value = jnp.where(first, total, total + pltpu.roll(error, 4, 1))

    place = lane - 8 * lax.broadcasted_iota(jnp.int32, (RHS, 128), 0)
    sums = [jnp.sum(jnp.where(place == q, value, 0.0), axis=1, keepdims=True) for q in range(8)]
    old, curve, cross, square = (settle((sums[q], sums[q + 4])) for q in range(4))
    step = old[0] / curve[0]
    change = scale_pair(square, -step)
    change = scale_pair(add_pairs((2.0 * cross[0], 2.0 * cross[1]), change), -step)
    new = settle(add_pairs(old, change))[0]
    fresh = residual - step * image
    new_sol_ref[...] = sol_ref[...] + step * direction
    new_res_ref[...] = fresh
    new_dir_ref[...] = fresh + new / old[0] * direction

    for copy in sends:
        copy.wait_send()

    def sent(i, carry):
        remote(send_a.at[i], back_a.at[i], ra_send.at[i], ra_recv.at[i], row_shift(1)).wait_send()
        return carry

    lax.fori_loop(0, len(every), sent, 0)


def solution(mesh):
    nr, nc = mesh.shape["row"], mesh.shape["col"]
    ny = 4 if nc == 32 else 2
    nz = nc // ny
    whole, half = offsets(nz, ny)
    na = len(whole) + len(half)

    def local(points, inv_length, solution_, residual, direction):
        width = points.shape[0]
        vmem = pl.BlockSpec(memory_space=pltpu.VMEM)
        dma = pltpu.SemaphoreType.DMA
        out = jax.ShapeDtypeStruct((RHS, width), F)
        flat = pl.pallas_call(
            functools.partial(kernel, (nr, nz, ny, whole, half)),
            out_shape=(out, out, out),
            in_specs=[pl.BlockSpec(memory_space=pltpu.HBM)] * 5,
            out_specs=(vmem, vmem, vmem),
            scratch_shapes=[
                pltpu.VMEM((DIM, width), F),
                pltpu.VMEM((1, DIM), F),
                pltpu.VMEM((RHS, width), F),
                pltpu.VMEM((RHS, width), F),
                pltpu.VMEM((RHS, width), F),
                pltpu.VMEM((PACK, width), F),
                pltpu.VMEM((na, PACK, width), F),
                pltpu.VMEM((nr, PACK, width), F),
                pltpu.VMEM((nr * width, DEPTH), H),
                pltpu.VMEM((2 * RHS, nr * width), H),
                pltpu.VMEM((nr * width, 2 * RHS), F),
                pltpu.VMEM((na, RHS, width), F),
                pltpu.VMEM((nr, RHS, width), F),
                pltpu.VMEM((na, RHS, width), F),
                pltpu.VMEM((nr, RHS, width), F),
                pltpu.VMEM((nr, 1, 128), F),
                pltpu.VMEM((nc, 1, 128), F),
                dma((5,)),
                dma((na,)), dma((na,)), dma((nr,)), dma((nr,)),
                dma((na,)), dma((na,)), dma((nr,)), dma((nr,)),
                dma((nr,)), dma((nr,)), dma((nc,)), dma((nc,)),
            ],
            compiler_params=pltpu.CompilerParams(
                collective_id=0, has_side_effects=True, vmem_limit_bytes=48 * 2**20
            ),
            cost_estimate=pl.CostEstimate(flops=2 * 10**10, bytes_accessed=10**6, transcendentals=2 * 10**7),
        )(points.T, inv_length.reshape(1, DIM), solution_.T, residual.T, direction.T)
        return tuple(x.T for x in flat)

    placed = (
        P(("row", "col"), None),
        P(),
        P(("row", "col"), None),
        P(("row", "col"), None),
        P(("row", "col"), None),
    )
    return jax.shard_map(
        local,
        mesh=mesh,
        in_specs=placed,
        out_specs=(P(("row", "col"), None),) * 3,
        check_vma=False,
    )
```

```python
import functools
import math

import jax
import jax.numpy as jnp
from jax import lax
from jax.experimental import pallas as pl
from jax.experimental.pallas import tpu as pltpu
from jax.sharding import PartitionSpec as P

F = jnp.float32
H = jnp.bfloat16
MESH = pl.DeviceIdType.MESH
noise_level = 0.1
LOG2E = 1.0 / math.log(2.0)
SCALE = math.sqrt(5.0) * LOG2E
C1 = 3.0 * LOG2E
C0 = 3.0 * LOG2E * LOG2E
GAIN = 1.0 / C0
DIM = 32
RHS = 8
PACK = DIM + RHS
DEPTH = 256


def offsets(nz, ny):
    def hop(d, n):
        return min(d, n - d)

    whole, half, load = [], [], {}
    every = sorted(
        ((dz, dy) for dz in range(nz) for dy in range(ny)),
        key=lambda o: (hop(o[0], nz) + hop(o[1], ny), o),
    )

    def charge(o):
        dz, dy = o
        out = {}
        if dz and 2 * dz != nz:
            out["z+" if 2 * dz < nz else "z-"] = hop(dz, nz)
        if dy and 2 * dy != ny:
            out["y+" if 2 * dy < ny else "y-"] = hop(dy, ny)
        return out

    for o in every:
        back = ((-o[0]) % nz, (-o[1]) % ny)
        if o == (0, 0):
            continue
        if o == back:
            half.append(o)
            continue
        if o in whole or back in whole:
            continue

        def cost(cand):
            trial = dict(load)
            for key, hops in charge(cand).items():
                trial[key] = trial.get(key, 0) + hops
            return sum(v * v for v in trial.values())

        pick = min((o, back), key=cost)
        for key, hops in charge(pick).items():
            load[key] = load.get(key, 0) + hops
        whole.append(pick)
    return whole, half


def pieces(x):
    first = x.astype(H).astype(F)
    rest = x - first
    second = rest.astype(H).astype(F)
    third = (rest - second).astype(H).astype(F)
    return first, second, third


def norms(scaled):
    return jnp.sum(scaled * scaled, axis=0, keepdims=True)


def stack_left(block, width):
    scaled = block[:DIM, :]
    h, m, l = pieces(scaled)
    qh, qm, ql = pieces(norms(scaled))
    one = jnp.ones((1, width), F)
    zero = jnp.zeros((DEPTH - 6 * DIM - 8, width), F)
    tail = jnp.concatenate([qh, qm, ql, one, one, one, zero[:2]], axis=0)
    return jnp.concatenate([h, h, m, m, h, l, tail, zero], axis=0)


def stack_right(block, width):
    scaled = block[:DIM, :]
    h, m, l = pieces(scaled)
    h, m, l = -2.0 * h, -2.0 * m, -2.0 * l
    qh, qm, ql = pieces(norms(scaled))
    one = jnp.ones((1, width), F)
    zero = jnp.zeros((DEPTH - 6 * DIM - 8, width), F)
    tail = jnp.concatenate([one, one, one, qh, qm, ql, zero[:2]], axis=0)
    return jnp.concatenate([h, m, h, m, l, h, tail, zero], axis=0)


def two_pieces(v):
    first = v.astype(H).astype(F)
    return jnp.concatenate([first, v - first], axis=0)


def matern(x):
    x = jnp.maximum(x, 1e-30)
    t = x * lax.rsqrt(x)
    return (t * (t + C1) + C0) * jnp.exp2(-t)


def two_sum(a, b):
    s = a + b
    t = s - a
    return s, (a - (s - t)) + (b - t)


def split(a):
    c = a * 4097.0
    high = c - (c - a)
    return high, a - high


def two_product(a, b):
    p = a * b
    ah, al = split(a)
    bh, bl = split(b)
    return p, ((ah * bh - p) + ah * bl + al * bh) + al * bl


def add_pairs(a, b):
    s, e = two_sum(a[0], b[0])
    return s, e + (a[1] + b[1])


def settle(a):
    return two_sum(a[0], a[1])


def scale_pair(a, f):
    p, e = two_product(a[0], f)
    return settle((p, e + a[1] * f))


def tree(items, join):
    while len(items) > 1:
        items = [join(*items[i:i + 2]) if i + 1 < len(items) else items[i] for i in range(0, len(items), 2)]
    return items[0]


def dot_pair(a, b):
    p, e = two_product(a, b)
    n = a.shape[1] // 128
    pair = tree([(p[:, i * 128:(i + 1) * 128], e[:, i * 128:(i + 1) * 128]) for i in range(n)], add_pairs)
    for shift in (64, 32, 16, 8, 4, 2, 1):
        pair = add_pairs(pair, tuple(pltpu.roll(x, shift, 1) for x in pair))
    return pair


def kernel(
    plan,
    pts_hbm, inv_hbm, sol_hbm, res_hbm, dir_hbm,
    out_ref,
    pts_ref, inv_ref, sol_ref, res_ref, dir_ref,
    pack, gather_a, gather_b, rows_b, vals_b, sums_b,
    send_a, send_b, back_a, back_b, red_row, red_col,
    in_sem, ga_send, ga_recv, gb_send, gb_recv, ra_send, ra_recv, rb_send, rb_recv,
    rr_send, rr_recv, rc_send, rc_recv,
):
    nr, nz, ny, whole, half = plan
    nx = nr // 2
    width = pts_ref.shape[1]
    r = lax.axis_index("row")
    c = lax.axis_index("col")
    z, y = c // ny, c % ny
    x, core = r // 2, r % 2
    every = whole + half

    def shift(dz, dy):
        return (r, lax.rem(z + dz, nz) * ny + lax.rem(y + dy, ny))

    def row_shift(o, sign=1):
        dx = (o // 2) if sign > 0 else (nx - o // 2) % nx
        return (lax.rem(x + dx, nx) * 2 + lax.rem(core + o % 2, 2), c)

    def opposite(o):
        return ((nz - o[0]) % nz, (ny - o[1]) % ny)

    def remote(src, dst, send_sem, recv_sem, device):
        return pltpu.make_async_remote_copy(
            src_ref=src, dst_ref=dst, send_sem=send_sem, recv_sem=recv_sem,
            device_id=device, device_id_type=MESH,
        )

    barrier = pltpu.get_barrier_semaphore()
    for o in every:
        pl.semaphore_signal(barrier, inc=1, device_id=shift(*opposite(o)), device_id_type=MESH)
    for o in range(1, nr):
        pl.semaphore_signal(barrier, inc=1, device_id=row_shift(o), device_id_type=MESH)

    loads = [
        pltpu.make_async_copy(src, dst, in_sem.at[i])
        for i, (src, dst) in enumerate((
            (pts_hbm, pts_ref), (dir_hbm, dir_ref), (inv_hbm, inv_ref), (res_hbm, res_ref), (sol_hbm, sol_ref),
        ))
    ]
    for copy in loads:
        copy.start()
    sums_b[...] = jnp.zeros_like(sums_b)
    for copy in loads:
        copy.wait()

    lengths = jnp.transpose(jnp.broadcast_to(inv_ref[...], (DIM, DIM)))[:, :1]
    pack[0:DIM, :] = pts_ref[...] * lengths * SCALE
    pack[DIM:PACK, :] = dir_ref[...]
    pl.semaphore_wait(barrier, len(every) + nr - 1)

    sends = []
    for o in range(1, nr):
        sends.append(remote(pack, gather_b.at[o], gb_send.at[o], gb_recv.at[o], row_shift(o, -1)))
    for i, o in enumerate(every):
        sends.append(remote(pack, gather_a.at[i], ga_send.at[i], ga_recv.at[i], shift(*o)))
    for copy in sends:
        copy.start()

    def prepare_b(o, block):
        at = pl.ds(pl.multiple_of(o * width, width), width)
        rows_b[at, :] = jnp.transpose(stack_right(block, width)).astype(H)
        vals_b[:, at] = two_pieces(block[DIM:PACK, :]).astype(H)

    prepare_b(0, pack[...])

    def arrive_b(o, carry):
        remote(pack, gather_b.at[o], gb_send.at[o], gb_recv.at[o], row_shift(1)).wait_recv()
        prepare_b(o, gather_b[o])
        return carry

    lax.fori_loop(1, nr, arrive_b, 0)

    def prepare_a(block):
        left = stack_left(block, width).astype(H)
        vals = jnp.transpose(two_pieces(block[DIM:PACK, :])).astype(H)
        return left, jnp.concatenate([vals, vals], axis=0)

    def strip(left, rows):
        k = matern(jnp.dot(rows, left, preferred_element_type=F))
        high = k.astype(H)
        low = (k - high.astype(F)).astype(H)
        return high, low

    def down(values, high, low):
        out = jnp.dot(
            jnp.concatenate([values, values], axis=1),
            jnp.concatenate([high, low], axis=0),
            preferred_element_type=F,
        )
        return out[:RHS] + out[RHS:]

    def across(high, low, vals):
        return jnp.dot(jnp.concatenate([high, low], axis=1), vals, preferred_element_type=F)

    def table(i, entries):
        out = jnp.int32(entries[0])
        for n in range(1, len(entries)):
            out = jnp.where(i == n, jnp.int32(entries[n]), out)
        return out

    def give_back(i, value, entries, base):
        send_a[i] = value
        back = [opposite(o) for o in entries]
        dz = table(i - base, [o[0] for o in back])
        dy = table(i - base, [o[1] for o in back])
        remote(send_a.at[i], back_a.at[i], ra_send.at[i], ra_recv.at[i], shift(dz, dy)).start()

    def whole_strip(i, carry):
        remote(pack, gather_a.at[i], ga_send.at[i], ga_recv.at[i], row_shift(1)).wait_recv()
        left, vals = prepare_a(gather_a[i])
        high, low = strip(left, rows_b[...])
        give_back(i, down(vals_b[...], high, low), whole, 0)
        sums_b[...] += across(high, low, vals)
        return carry

    lax.fori_loop(0, len(whole), whole_strip, 0)

    halves = []
    for dz, dy in half:
        halves.append(2 * z // nz if dz else 2 * y // ny)

    def half_strip(i, carry):
        n = i - len(whole)
        remote(pack, gather_a.at[i], ga_send.at[i], ga_recv.at[i], row_shift(1)).wait_recv()
        left, vals = prepare_a(gather_a[i])
        side = halves[0]
        for k in range(1, len(halves)):
            side = jnp.where(n == k, halves[k], side)
        at = pl.ds(pl.multiple_of((1 - side) * 2 * width, 2 * width), nr // 2 * width)
        high, low = strip(left, rows_b[at, :])
        give_back(i, down(vals_b[:, at], high, low), half, len(whole))
        sums_b[at, :] += across(high, low, vals)
        return carry

    lax.fori_loop(len(whole), len(every), half_strip, 0)

    for o in range(1, nr):
        flipped = jnp.transpose(sums_b[o * width:(o + 1) * width, :])
        send_b[o] = flipped[:RHS] + flipped[RHS:]
        copy = remote(send_b.at[o], back_b.at[o], rb_send.at[o], rb_recv.at[o], row_shift(o))
        copy.start()
        sends.append(copy)
    flipped = jnp.transpose(sums_b[0:width, :])
    image = flipped[:RHS] + flipped[RHS:]

    left, _ = prepare_a(pack[...])
    high, low = strip(left, rows_b[...])
    image = image + down(vals_b[...], high, low)

    for i in range(len(every)):
        copy = remote(send_a.at[i], back_a.at[i], ra_send.at[i], ra_recv.at[i], row_shift(1))
        copy.wait_recv()
        image = image + back_a[i]
    for o in range(1, nr):
        remote(send_b.at[o], back_b.at[o], rb_send.at[o], rb_recv.at[o], row_shift(1)).wait_recv()
        image = image + back_b[o]

    direction = dir_ref[...]
    residual = res_ref[...]
    image = GAIN * image + noise_level * direction

    lane = lax.broadcasted_iota(jnp.int32, (RHS, 128), 1)
    pairs = [dot_pair(residual, residual), dot_pair(direction, image), dot_pair(residual, image), dot_pair(image, image)]
    mixed = jnp.zeros((RHS, 128), F)
    for q, pair in enumerate(pairs):
        mixed = jnp.where(lane == q, pair[0], jnp.where(lane == q + 4, pair[1], mixed))
    value = jnp.sum(pltpu.roll(mixed, 0, 1, stride=8, stride_axis=0), axis=0, keepdims=True)
    first = lax.broadcasted_iota(jnp.int32, (1, 128), 1) % 8 < 4

    for size, buf, ssem, rsem, mine, peer in (
        (nr, red_row, rr_send, rr_recv, r, lambda e: (lax.rem(r + e, nr), c)),
        (nz * ny, red_col, rc_send, rc_recv, c, lambda e: (r, lax.rem(c + e, nz * ny))),
    ):
        buf[mine] = value
        for e in range(1, size):
            copy = remote(buf.at[mine], buf.at[mine], ssem.at[e], rsem.at[mine], peer(e))
            copy.start()
            sends.append(copy)
        for e in range(1, size):
            other = lax.rem(mine + e, size)
            remote(buf.at[other], buf.at[other], ssem.at[e], rsem.at[other], peer(e)).wait_recv()
        total, error = tree([(buf[e], jnp.zeros((1, 128), F)) for e in range(size)], add_pairs)
        value = jnp.where(first, total, total + pltpu.roll(error, 4, 1))

    place = lane - 8 * lax.broadcasted_iota(jnp.int32, (RHS, 128), 0)
    sums = [jnp.sum(jnp.where(place == q, value, 0.0), axis=1, keepdims=True) for q in range(8)]
    old, curve, cross, square = (settle((sums[q], sums[q + 4])) for q in range(4))
    step = old[0] / curve[0]
    change = scale_pair(square, -step)
    change = scale_pair(add_pairs((2.0 * cross[0], 2.0 * cross[1]), change), -step)
    new = settle(add_pairs(old, change))[0]
    fresh = residual - step * image
    out_ref[0:8] = sol_ref[...] + step * direction
    out_ref[8:16] = fresh
    out_ref[16:24] = fresh + new / old[0] * direction

    for copy in sends:
        copy.wait_send()

    def sent(i, carry):
        remote(send_a.at[i], back_a.at[i], ra_send.at[i], ra_recv.at[i], row_shift(1)).wait_send()
        return carry

    lax.fori_loop(0, len(every), sent, 0)


def solution(mesh):
    nr, nc = mesh.shape["row"], mesh.shape["col"]
    ny = 4 if nc == 32 else 2
    nz = nc // ny
    whole, half = offsets(nz, ny)
    na = len(whole) + len(half)

    def local(points, inv_length, solution_, residual, direction):
        width = points.shape[0]
        vmem = pl.BlockSpec(memory_space=pltpu.VMEM)
        dma = pltpu.SemaphoreType.DMA
        out = jax.ShapeDtypeStruct((3 * RHS, width), F)
        flat = pl.pallas_call(
            functools.partial(kernel, (nr, nz, ny, whole, half)),
            out_shape=out,
            in_specs=[pl.BlockSpec(memory_space=pltpu.HBM)] * 5,
            out_specs=vmem,
            scratch_shapes=[
                pltpu.VMEM((DIM, width), F),
                pltpu.VMEM((1, DIM), F),
                pltpu.VMEM((RHS, width), F),
                pltpu.VMEM((RHS, width), F),
                pltpu.VMEM((RHS, width), F),
                pltpu.VMEM((PACK, width), F),
                pltpu.VMEM((na, PACK, width), F),
                pltpu.VMEM((nr, PACK, width), F),
                pltpu.VMEM((nr * width, DEPTH), H),
                pltpu.VMEM((2 * RHS, nr * width), H),
                pltpu.VMEM((nr * width, 2 * RHS), F),
                pltpu.VMEM((na, RHS, width), F),
                pltpu.VMEM((nr, RHS, width), F),
                pltpu.VMEM((na, RHS, width), F),
                pltpu.VMEM((nr, RHS, width), F),
                pltpu.VMEM((nr, 1, 128), F),
                pltpu.VMEM((nc, 1, 128), F),
                dma((5,)),
                dma((na,)), dma((na,)), dma((nr,)), dma((nr,)),
                dma((na,)), dma((na,)), dma((nr,)), dma((nr,)),
                dma((nr,)), dma((nr,)), dma((nc,)), dma((nc,)),
            ],
            compiler_params=pltpu.CompilerParams(
                collective_id=0, has_side_effects=True
            ),
            cost_estimate=pl.CostEstimate(flops=2 * 10**10, bytes_accessed=10**6, transcendentals=2 * 10**7),
        )(points.T, inv_length.reshape(1, DIM), solution_.T, residual.T, direction.T)
        return flat[0:8].T, flat[8:16].T, flat[16:24].T

    placed = (
        P(("row", "col"), None),
        P(),
        P(("row", "col"), None),
        P(("row", "col"), None),
        P(("row", "col"), None),
    )
    return jax.shard_map(
        local,
        mesh=mesh,
        in_specs=placed,
        out_specs=(P(("row", "col"), None),) * 3,
        check_vma=False,
    )
```

```python
import functools
import math

import jax
import jax.numpy as jnp
from jax import lax
from jax.experimental import pallas as pl
from jax.experimental.pallas import tpu as pltpu
from jax.sharding import PartitionSpec as P

F = jnp.float32
H = jnp.bfloat16
MESH = pl.DeviceIdType.MESH
noise_level = 0.1
LOG2E = 1.0 / math.log(2.0)
SCALE = math.sqrt(5.0) * LOG2E
C1 = 3.0 * LOG2E
C0 = 3.0 * LOG2E * LOG2E
GAIN = 1.0 / C0
DIM = 32
RHS = 8
PACK = DIM + RHS
NEAR = 2
DEPTH = 256


def offsets(nz, ny):
    def hop(d, n):
        return min(d, n - d)

    whole, half, load = [], [], {}
    every = sorted(
        ((dz, dy) for dz in range(nz) for dy in range(ny)),
        key=lambda o: (hop(o[0], nz) + hop(o[1], ny), o),
    )

    def charge(o):
        dz, dy = o
        out = {}
        if dz and 2 * dz != nz:
            out["z+" if 2 * dz < nz else "z-"] = hop(dz, nz)
        if dy and 2 * dy != ny:
            out["y+" if 2 * dy < ny else "y-"] = hop(dy, ny)
        return out

    for o in every:
        back = ((-o[0]) % nz, (-o[1]) % ny)
        if o == (0, 0):
            continue
        if o == back:
            half.append(o)
            continue
        if o in whole or back in whole:
            continue

        def cost(cand):
            trial = dict(load)
            for key, hops in charge(cand).items():
                trial[key] = trial.get(key, 0) + hops
            return sum(v * v for v in trial.values())

        pick = min((o, back), key=cost)
        for key, hops in charge(pick).items():
            load[key] = load.get(key, 0) + hops
        whole.append(pick)
    return whole, half


def pieces(x):
    first = x.astype(H).astype(F)
    rest = x - first
    second = rest.astype(H).astype(F)
    third = (rest - second).astype(H).astype(F)
    return first, second, third


def norms(scaled):
    return jnp.sum(scaled * scaled, axis=0, keepdims=True)


def stack_left(block, width):
    scaled = block[:DIM, :]
    h, m, l = pieces(scaled)
    qh, qm, ql = pieces(norms(scaled))
    one = jnp.ones((1, width), F)
    zero = jnp.zeros((DEPTH - 6 * DIM - 8, width), F)
    tail = jnp.concatenate([qh, qm, ql, one, one, one, zero[:2]], axis=0)
    return jnp.concatenate([h, h, m, m, h, l, tail, zero], axis=0)


def stack_right(block, width):
    scaled = block[:DIM, :]
    h, m, l = pieces(scaled)
    h, m, l = -2.0 * h, -2.0 * m, -2.0 * l
    qh, qm, ql = pieces(norms(scaled))
    one = jnp.ones((1, width), F)
    zero = jnp.zeros((DEPTH - 6 * DIM - 8, width), F)
    tail = jnp.concatenate([one, one, one, qh, qm, ql, zero[:2]], axis=0)
    return jnp.concatenate([h, m, h, m, l, h, tail, zero], axis=0)


def two_pieces(v):
    first = v.astype(H).astype(F)
    return jnp.concatenate([first, v - first], axis=0)


def matern(x):
    x = jnp.maximum(x, 1e-30)
    t = x * lax.rsqrt(x)
    return (t * (t + C1) + C0) * jnp.exp2(-t)


def two_sum(a, b):
    s = a + b
    t = s - a
    return s, (a - (s - t)) + (b - t)


def split(a):
    c = a * 4097.0
    high = c - (c - a)
    return high, a - high


def two_product(a, b):
    p = a * b
    ah, al = split(a)
    bh, bl = split(b)
    return p, ((ah * bh - p) + ah * bl + al * bh) + al * bl


def add_pairs(a, b):
    s, e = two_sum(a[0], b[0])
    return s, e + (a[1] + b[1])


def settle(a):
    return two_sum(a[0], a[1])


def scale_pair(a, f):
    p, e = two_product(a[0], f)
    return settle((p, e + a[1] * f))


def tree(items, join):
    while len(items) > 1:
        items = [join(*items[i:i + 2]) if i + 1 < len(items) else items[i] for i in range(0, len(items), 2)]
    return items[0]


def dot_pair(a, b):
    p, e = two_product(a, b)
    n = a.shape[1] // 128
    pair = tree([(p[:, i * 128:(i + 1) * 128], e[:, i * 128:(i + 1) * 128]) for i in range(n)], add_pairs)
    for shift in (64, 32, 16, 8, 4, 2, 1):
        pair = add_pairs(pair, tuple(pltpu.roll(x, shift, 1) for x in pair))
    return pair


def kernel(
    plan,
    pts_hbm, inv_hbm, sol_hbm, res_hbm, dir_hbm,
    out_ref,
    pts_ref, inv_ref, sol_ref, res_ref, dir_ref,
    pack, gather_a, gather_b, rows_b, vals_b, sums_b,
    send_a, send_b, back_a, back_b, red_row, red_col,
    in_sem, ga_send, ga_recv, gb_send, gb_recv, ra_send, ra_recv, rb_send, rb_recv,
    rr_send, rr_recv, rc_send, rc_recv,
):
    nr, nz, ny, whole, half = plan
    nx = nr // 2
    width = pts_ref.shape[1]
    r = lax.axis_index("row")
    c = lax.axis_index("col")
    z, y = c // ny, c % ny
    x, core = r // 2, r % 2
    every = whole + half

    def shift(dz, dy):
        return (r, lax.rem(z + dz, nz) * ny + lax.rem(y + dy, ny))

    def row_shift(o, sign=1):
        dx = (o // 2) if sign > 0 else (nx - o // 2) % nx
        return (lax.rem(x + dx, nx) * 2 + lax.rem(core + o % 2, 2), c)

    def opposite(o):
        return ((nz - o[0]) % nz, (ny - o[1]) % ny)

    def remote(src, dst, send_sem, recv_sem, device):
        return pltpu.make_async_remote_copy(
            src_ref=src, dst_ref=dst, send_sem=send_sem, recv_sem=recv_sem,
            device_id=device, device_id_type=MESH,
        )

    barrier = pltpu.get_barrier_semaphore()
    for o in every:
        pl.semaphore_signal(barrier, inc=1, device_id=shift(*opposite(o)), device_id_type=MESH)
    for o in range(1, nr):
        pl.semaphore_signal(barrier, inc=1, device_id=row_shift(o), device_id_type=MESH)

    loads = [
        pltpu.make_async_copy(src, dst, in_sem.at[i])
        for i, (src, dst) in enumerate((
            (pts_hbm, pts_ref), (dir_hbm, dir_ref), (inv_hbm, inv_ref), (res_hbm, res_ref), (sol_hbm, sol_ref),
        ))
    ]
    for copy in loads:
        copy.start()
    sums_b[...] = jnp.zeros_like(sums_b)
    for copy in loads:
        copy.wait()

    lengths = jnp.transpose(jnp.broadcast_to(inv_ref[...], (DIM, DIM)))[:, :1]
    pack[0:DIM, :] = pts_ref[...] * lengths * SCALE
    pack[DIM:PACK, :] = dir_ref[...]
    pl.semaphore_wait(barrier, len(every) + nr - 1)

    to_row = [
        remote(pack, gather_b.at[o], gb_send.at[o], gb_recv.at[o], row_shift(o, -1)) for o in range(1, nr)
    ]
    to_col = [
        remote(pack, gather_a.at[i], ga_send.at[i], ga_recv.at[i], shift(*o)) for i, o in enumerate(every)
    ]
    sends = to_row[:1] + to_col[:2] + to_row[1:] + to_col[2:]
    for copy in sends:
        copy.start()

    def prepare_b(o, block):
        at = pl.ds(pl.multiple_of(o * width, width), width)
        rows_b[at, :] = jnp.transpose(stack_right(block, width)).astype(H)
        vals_b[:, at] = two_pieces(block[DIM:PACK, :]).astype(H)

    prepare_b(0, pack[...])

    def arrive_b(o, carry):
        remote(pack, gather_b.at[o], gb_send.at[o], gb_recv.at[o], row_shift(1)).wait_recv()
        prepare_b(o, gather_b[o])
        return carry

    arrive_b(1, 0)

    def prepare_a(block):
        left = stack_left(block, width).astype(H)
        vals = jnp.transpose(two_pieces(block[DIM:PACK, :])).astype(H)
        return left, jnp.concatenate([vals, vals], axis=0)

    def strip(left, rows):
        k = matern(jnp.dot(rows, left, preferred_element_type=F))
        high = k.astype(H)
        low = (k - high.astype(F)).astype(H)
        return high, low

    def down(values, high, low):
        out = jnp.dot(
            jnp.concatenate([values, values], axis=1),
            jnp.concatenate([high, low], axis=0),
            preferred_element_type=F,
        )
        return out[:RHS] + out[RHS:]

    def across(high, low, vals):
        return jnp.dot(jnp.concatenate([high, low], axis=1), vals, preferred_element_type=F)

    def table(i, entries):
        out = jnp.int32(entries[0])
        for n in range(1, len(entries)):
            out = jnp.where(i == n, jnp.int32(entries[n]), out)
        return out

    def give_back(i, value, entries, base):
        send_a[i] = value
        back = [opposite(o) for o in entries]
        dz = table(i - base, [o[0] for o in back])
        dy = table(i - base, [o[1] for o in back])
        remote(send_a.at[i], back_a.at[i], ra_send.at[i], ra_recv.at[i], shift(dz, dy)).start()

    def work(i, at):
        left, vals = prepare_a(gather_a[i])
        high, low = strip(left, rows_b[at, :])
        sums_b[at, :] += across(high, low, vals)
        return down(vals_b[:, at], high, low)

    def arrive_a(i):
        remote(pack, gather_a.at[i], ga_send.at[i], ga_recv.at[i], row_shift(1)).wait_recv()

    near = min(NEAR, len(whole))
    chip, rest = slice(0, 2 * width), slice(2 * width, nr * width)

    def near_strip(i, carry):
        arrive_a(i)
        send_a[i] = work(i, chip)
        return carry

    def whole_strip(i, carry):
        arrive_a(i)
        give_back(i, work(i, slice(None)), whole, 0)
        return carry

    def last_strip(i, carry):
        give_back(i, send_a[i] + work(i, rest), whole, 0)
        return carry

    lax.fori_loop(0, near, near_strip, 0)
    lax.fori_loop(2, nr, arrive_b, 0)
    lax.fori_loop(near, len(whole), whole_strip, 0)

    halves = []
    for dz, dy in half:
        halves.append(2 * z // nz if dz else 2 * y // ny)

    def half_strip(i, carry):
        n = i - len(whole)
        arrive_a(i)
        side = halves[0]
        for k in range(1, len(halves)):
            side = jnp.where(n == k, halves[k], side)
        at = pl.ds(pl.multiple_of((1 - side) * 2 * width, 2 * width), nr // 2 * width)
        give_back(i, work(i, at), half, len(whole))
        return carry

    lax.fori_loop(len(whole), len(every), half_strip, 0)
    lax.fori_loop(0, near, last_strip, 0)

    for o in range(1, nr):
        flipped = jnp.transpose(sums_b[o * width:(o + 1) * width, :])
        send_b[o] = flipped[:RHS] + flipped[RHS:]
        copy = remote(send_b.at[o], back_b.at[o], rb_send.at[o], rb_recv.at[o], row_shift(o))
        copy.start()
        sends.append(copy)
    flipped = jnp.transpose(sums_b[0:width, :])
    image = flipped[:RHS] + flipped[RHS:]

    left, _ = prepare_a(pack[...])
    high, low = strip(left, rows_b[...])
    image = image + down(vals_b[...], high, low)

    for i in range(len(every)):
        copy = remote(send_a.at[i], back_a.at[i], ra_send.at[i], ra_recv.at[i], row_shift(1))
        copy.wait_recv()
        image = image + back_a[i]
    for o in range(1, nr):
        remote(send_b.at[o], back_b.at[o], rb_send.at[o], rb_recv.at[o], row_shift(1)).wait_recv()
        image = image + back_b[o]

    direction = dir_ref[...]
    residual = res_ref[...]
    image = GAIN * image + noise_level * direction

    lane = lax.broadcasted_iota(jnp.int32, (RHS, 128), 1)
    pairs = [dot_pair(residual, residual), dot_pair(direction, image), dot_pair(residual, image), dot_pair(image, image)]
    mixed = jnp.zeros((RHS, 128), F)
    for q, pair in enumerate(pairs):
        mixed = jnp.where(lane == q, pair[0], jnp.where(lane == q + 4, pair[1], mixed))
    value = jnp.sum(pltpu.roll(mixed, 0, 1, stride=8, stride_axis=0), axis=0, keepdims=True)
    first = lax.broadcasted_iota(jnp.int32, (1, 128), 1) % 8 < 4

    for size, buf, ssem, rsem, mine, peer in (
        (nr, red_row, rr_send, rr_recv, r, lambda e: (lax.rem(r + e, nr), c)),
        (nz * ny, red_col, rc_send, rc_recv, c, lambda e: (r, lax.rem(c + e, nz * ny))),
    ):
        buf[mine] = value
        for e in range(1, size):
            copy = remote(buf.at[mine], buf.at[mine], ssem.at[e], rsem.at[mine], peer(e))
            copy.start()
            sends.append(copy)
        for e in range(1, size):
            other = lax.rem(mine + e, size)
            remote(buf.at[other], buf.at[other], ssem.at[e], rsem.at[other], peer(e)).wait_recv()
        total, error = tree([(buf[e], jnp.zeros((1, 128), F)) for e in range(size)], add_pairs)
        value = jnp.where(first, total, total + pltpu.roll(error, 4, 1))

    place = lane - 8 * lax.broadcasted_iota(jnp.int32, (RHS, 128), 0)
    sums = [jnp.sum(jnp.where(place == q, value, 0.0), axis=1, keepdims=True) for q in range(8)]
    old, curve, cross, square = (settle((sums[q], sums[q + 4])) for q in range(4))
    step = old[0] / curve[0]
    change = scale_pair(square, -step)
    change = scale_pair(add_pairs((2.0 * cross[0], 2.0 * cross[1]), change), -step)
    new = settle(add_pairs(old, change))[0]
    fresh = residual - step * image
    out_ref[0:8] = sol_ref[...] + step * direction
    out_ref[8:16] = fresh
    out_ref[16:24] = fresh + new / old[0] * direction

    for copy in sends:
        copy.wait_send()

    def sent(i, carry):
        remote(send_a.at[i], back_a.at[i], ra_send.at[i], ra_recv.at[i], row_shift(1)).wait_send()
        return carry

    lax.fori_loop(0, len(every), sent, 0)


def solution(mesh):
    nr, nc = mesh.shape["row"], mesh.shape["col"]
    ny = 4 if nc == 32 else 2
    nz = nc // ny
    whole, half = offsets(nz, ny)
    na = len(whole) + len(half)

    def local(points, inv_length, solution_, residual, direction):
        width = points.shape[0]
        vmem = pl.BlockSpec(memory_space=pltpu.VMEM)
        dma = pltpu.SemaphoreType.DMA
        out = jax.ShapeDtypeStruct((3 * RHS, width), F)
        flat = pl.pallas_call(
            functools.partial(kernel, (nr, nz, ny, whole, half)),
            out_shape=out,
            in_specs=[pl.BlockSpec(memory_space=pltpu.HBM)] * 5,
            out_specs=vmem,
            scratch_shapes=[
                pltpu.VMEM((DIM, width), F),
                pltpu.VMEM((1, DIM), F),
                pltpu.VMEM((RHS, width), F),
                pltpu.VMEM((RHS, width), F),
                pltpu.VMEM((RHS, width), F),
                pltpu.VMEM((PACK, width), F),
                pltpu.VMEM((na, PACK, width), F),
                pltpu.VMEM((nr, PACK, width), F),
                pltpu.VMEM((nr * width, DEPTH), H),
                pltpu.VMEM((2 * RHS, nr * width), H),
                pltpu.VMEM((nr * width, 2 * RHS), F),
                pltpu.VMEM((na, RHS, width), F),
                pltpu.VMEM((nr, RHS, width), F),
                pltpu.VMEM((na, RHS, width), F),
                pltpu.VMEM((nr, RHS, width), F),
                pltpu.VMEM((nr, 1, 128), F),
                pltpu.VMEM((nc, 1, 128), F),
                dma((5,)),
                dma((na,)), dma((na,)), dma((nr,)), dma((nr,)),
                dma((na,)), dma((na,)), dma((nr,)), dma((nr,)),
                dma((nr,)), dma((nr,)), dma((nc,)), dma((nc,)),
            ],
            compiler_params=pltpu.CompilerParams(
                collective_id=0, has_side_effects=True
            ),
            cost_estimate=pl.CostEstimate(flops=2 * 10**10, bytes_accessed=10**6, transcendentals=2 * 10**7),
        )(points.T, inv_length.reshape(1, DIM), solution_.T, residual.T, direction.T)
        return flat[0:8].T, flat[8:16].T, flat[16:24].T

    placed = (
        P(("row", "col"), None),
        P(),
        P(("row", "col"), None),
        P(("row", "col"), None),
        P(("row", "col"), None),
    )
    return jax.shard_map(
        local,
        mesh=mesh,
        in_specs=placed,
        out_specs=(P(("row", "col"), None),) * 3,
        check_vma=False,
    )
```

```python
import functools
import math

import jax
import jax.numpy as jnp
from jax import lax
from jax.experimental import pallas as pl
from jax.experimental.pallas import tpu as pltpu
from jax.sharding import PartitionSpec as P

F = jnp.float32
H = jnp.bfloat16
Q = jnp.float8_e4m3fn
MESH = pl.DeviceIdType.MESH
noise_level = 0.1
LOG2E = 1.0 / math.log(2.0)
SCALE = math.sqrt(5.0) * LOG2E
C1 = 3.0 * LOG2E
C0 = 3.0 * LOG2E * LOG2E
LIFT = 14.0
GAIN = 2.0 ** -LIFT / C0
DIM = 32
RHS = 8
PACK = DIM + RHS
NEAR = 2
DEPTH = 256


def offsets(nz, ny):
    def hop(d, n):
        return min(d, n - d)

    whole, half, load = [], [], {}
    every = sorted(
        ((dz, dy) for dz in range(nz) for dy in range(ny)),
        key=lambda o: (hop(o[0], nz) + hop(o[1], ny), o),
    )

    def charge(o):
        dz, dy = o
        out = {}
        if dz and 2 * dz != nz:
            out["z+" if 2 * dz < nz else "z-"] = hop(dz, nz)
        if dy and 2 * dy != ny:
            out["y+" if 2 * dy < ny else "y-"] = hop(dy, ny)
        return out

    for o in every:
        back = ((-o[0]) % nz, (-o[1]) % ny)
        if o == (0, 0):
            continue
        if o == back:
            half.append(o)
            continue
        if o in whole or back in whole:
            continue

        def cost(cand):
            trial = dict(load)
            for key, hops in charge(cand).items():
                trial[key] = trial.get(key, 0) + hops
            return sum(v * v for v in trial.values())

        pick = min((o, back), key=cost)
        for key, hops in charge(pick).items():
            load[key] = load.get(key, 0) + hops
        whole.append(pick)
    return whole, half


def pieces(x):
    first = x.astype(H).astype(F)
    rest = x - first
    second = rest.astype(H).astype(F)
    third = (rest - second).astype(H).astype(F)
    return first, second, third


def norms(scaled):
    return jnp.sum(scaled * scaled, axis=0, keepdims=True)


def stack_left(block, width):
    scaled = block[:DIM, :]
    h, m, l = pieces(scaled)
    qh, qm, ql = pieces(norms(scaled))
    one = jnp.ones((1, width), F)
    zero = jnp.zeros((DEPTH - 6 * DIM - 8, width), F)
    tail = jnp.concatenate([qh, qm, ql, one, one, one, zero[:2]], axis=0)
    return jnp.concatenate([h, h, m, m, h, l, tail, zero], axis=0)


def stack_right(block, width):
    scaled = block[:DIM, :]
    h, m, l = pieces(scaled)
    h, m, l = -2.0 * h, -2.0 * m, -2.0 * l
    qh, qm, ql = pieces(norms(scaled))
    one = jnp.ones((1, width), F)
    zero = jnp.zeros((DEPTH - 6 * DIM - 8, width), F)
    tail = jnp.concatenate([one, one, one, qh, qm, ql, zero[:2]], axis=0)
    return jnp.concatenate([h, m, h, m, l, h, tail, zero], axis=0)


def two_pieces(v):
    first = v.astype(H).astype(F)
    return jnp.concatenate([first, v - first], axis=0)


def two_eighths(v):
    first = v.astype(Q).astype(F)
    return jnp.concatenate([first, v - first, jnp.zeros_like(v), jnp.zeros_like(v)], axis=0)


def matern(x):
    x = jnp.maximum(x, 1e-30)
    t = x * lax.rsqrt(x)
    return (t * (t + C1) + C0) * jnp.exp2(LIFT - t)


def two_sum(a, b):
    s = a + b
    t = s - a
    return s, (a - (s - t)) + (b - t)


def split(a):
    c = a * 4097.0
    high = c - (c - a)
    return high, a - high


def two_product(a, b):
    p = a * b
    ah, al = split(a)
    bh, bl = split(b)
    return p, ((ah * bh - p) + ah * bl + al * bh) + al * bl


def add_pairs(a, b):
    s, e = two_sum(a[0], b[0])
    return s, e + (a[1] + b[1])


def settle(a):
    return two_sum(a[0], a[1])


def scale_pair(a, f):
    p, e = two_product(a[0], f)
    return settle((p, e + a[1] * f))


def tree(items, join):
    while len(items) > 1:
        items = [join(*items[i:i + 2]) if i + 1 < len(items) else items[i] for i in range(0, len(items), 2)]
    return items[0]


def dot_pair(a, b):
    p, e = two_product(a, b)
    n = a.shape[1] // 128
    pair = tree([(p[:, i * 128:(i + 1) * 128], e[:, i * 128:(i + 1) * 128]) for i in range(n)], add_pairs)
    for shift in (64, 32, 16, 8, 4, 2, 1):
        pair = add_pairs(pair, tuple(pltpu.roll(x, shift, 1) for x in pair))
    return pair


def kernel(
    plan,
    pts_hbm, inv_hbm, sol_hbm, res_hbm, dir_hbm,
    out_ref,
    pts_ref, inv_ref, sol_ref, res_ref, dir_ref,
    pack, gather_a, gather_b, rows_b, vals_b, eighth_b, sums_b,
    send_a, send_b, back_a, back_b, red_row, red_col,
    in_sem, ga_send, ga_recv, gb_send, gb_recv, ra_send, ra_recv, rb_send, rb_recv,
    rr_send, rr_recv, rc_send, rc_recv,
):
    nr, nz, ny, whole, half = plan
    nx = nr // 2
    width = pts_ref.shape[1]
    r = lax.axis_index("row")
    c = lax.axis_index("col")
    z, y = c // ny, c % ny
    x, core = r // 2, r % 2
    every = whole + half

    def shift(dz, dy):
        return (r, lax.rem(z + dz, nz) * ny + lax.rem(y + dy, ny))

    def row_shift(o, sign=1):
        dx = (o // 2) if sign > 0 else (nx - o // 2) % nx
        return (lax.rem(x + dx, nx) * 2 + lax.rem(core + o % 2, 2), c)

    def opposite(o):
        return ((nz - o[0]) % nz, (ny - o[1]) % ny)

    def remote(src, dst, send_sem, recv_sem, device):
        return pltpu.make_async_remote_copy(
            src_ref=src, dst_ref=dst, send_sem=send_sem, recv_sem=recv_sem,
            device_id=device, device_id_type=MESH,
        )

    barrier = pltpu.get_barrier_semaphore()
    for o in every:
        pl.semaphore_signal(barrier, inc=1, device_id=shift(*opposite(o)), device_id_type=MESH)
    for o in range(1, nr):
        pl.semaphore_signal(barrier, inc=1, device_id=row_shift(o), device_id_type=MESH)

    loads = [
        pltpu.make_async_copy(src, dst, in_sem.at[i])
        for i, (src, dst) in enumerate((
            (pts_hbm, pts_ref), (dir_hbm, dir_ref), (inv_hbm, inv_ref), (res_hbm, res_ref), (sol_hbm, sol_ref),
        ))
    ]
    for copy in loads:
        copy.start()
    sums_b[...] = jnp.zeros_like(sums_b)
    for copy in loads:
        copy.wait()

    lengths = jnp.transpose(jnp.broadcast_to(inv_ref[...], (DIM, DIM)))[:, :1]
    pack[0:DIM, :] = pts_ref[...] * lengths * SCALE
    pack[DIM:PACK, :] = dir_ref[...]
    pl.semaphore_wait(barrier, len(every) + nr - 1)

    to_row = [
        remote(pack, gather_b.at[o], gb_send.at[o], gb_recv.at[o], row_shift(o, -1)) for o in range(1, nr)
    ]
    to_col = [
        remote(pack, gather_a.at[i], ga_send.at[i], ga_recv.at[i], shift(*o)) for i, o in enumerate(every)
    ]
    sends = to_row[:1] + to_col[:2] + to_row[1:] + to_col[2:]
    for copy in sends:
        copy.start()

    def prepare_b(o, block):
        at = pl.ds(pl.multiple_of(o * width, width), width)
        rows_b[at, :] = jnp.transpose(stack_right(block, width)).astype(H)
        vals_b[:, at] = two_pieces(block[DIM:PACK, :]).astype(H)
        eighth_b[:, at] = two_eighths(block[DIM:PACK, :]).astype(Q)

    prepare_b(0, pack[...])

    def arrive_b(o, carry):
        remote(pack, gather_b.at[o], gb_send.at[o], gb_recv.at[o], row_shift(1)).wait_recv()
        prepare_b(o, gather_b[o])
        return carry

    arrive_b(1, 0)

    def prepare_a(block):
        left = stack_left(block, width).astype(H)
        vals = jnp.transpose(two_pieces(block[DIM:PACK, :])).astype(H)
        eighth = jnp.transpose(two_eighths(block[DIM:PACK, :])[:2 * RHS]).astype(Q)
        return left, vals, eighth

    def strip(left, rows):
        k = matern(jnp.dot(rows, left, preferred_element_type=F))
        high = k.astype(H)
        low = (k - high.astype(F)).astype(Q)
        return high, low

    def product(a, b):
        return jnp.dot(a, b, preferred_element_type=F)

    def table(i, entries):
        out = jnp.int32(entries[0])
        for n in range(1, len(entries)):
            out = jnp.where(i == n, jnp.int32(entries[n]), out)
        return out

    def give_back(i, value, entries, base):
        send_a[i] = value
        back = [opposite(o) for o in entries]
        dz = table(i - base, [o[0] for o in back])
        dy = table(i - base, [o[1] for o in back])
        remote(send_a.at[i], back_a.at[i], ra_send.at[i], ra_recv.at[i], shift(dz, dy)).start()

    def work(i, at):
        left, vals, eighth = prepare_a(gather_a[i])
        high, low = strip(left, rows_b[at, :])
        sums_b[at, :] += product(high, vals)
        out = product(vals_b[:, at], high)
        sums_b[at, :] += product(low, eighth)
        fine = product(eighth_b[:, at], low)
        return out[:RHS] + out[RHS:] + (fine[:RHS] + fine[RHS:2 * RHS])

    def arrive_a(i):
        remote(pack, gather_a.at[i], ga_send.at[i], ga_recv.at[i], row_shift(1)).wait_recv()

    near = min(NEAR, len(whole))
    chip, rest = slice(0, 2 * width), slice(2 * width, nr * width)

    def near_strip(i, carry):
        arrive_a(i)
        send_a[i] = work(i, chip)
        return carry

    def whole_strip(i, carry):
        arrive_a(i)
        give_back(i, work(i, slice(None)), whole, 0)
        return carry

    def last_strip(i, carry):
        give_back(i, send_a[i] + work(i, rest), whole, 0)
        return carry

    lax.fori_loop(0, near, near_strip, 0)
    lax.fori_loop(2, nr, arrive_b, 0)
    lax.fori_loop(near, len(whole), whole_strip, 0)

    halves = []
    for dz, dy in half:
        halves.append(2 * z // nz if dz else 2 * y // ny)

    def half_strip(i, carry):
        n = i - len(whole)
        arrive_a(i)
        side = halves[0]
        for k in range(1, len(halves)):
            side = jnp.where(n == k, halves[k], side)
        at = pl.ds(pl.multiple_of((1 - side) * 2 * width, 2 * width), nr // 2 * width)
        give_back(i, work(i, at), half, len(whole))
        return carry

    lax.fori_loop(len(whole), len(every), half_strip, 0)
    lax.fori_loop(0, near, last_strip, 0)

    for o in range(1, nr):
        flipped = jnp.transpose(sums_b[o * width:(o + 1) * width, :])
        send_b[o] = flipped[:RHS] + flipped[RHS:]
        copy = remote(send_b.at[o], back_b.at[o], rb_send.at[o], rb_recv.at[o], row_shift(o))
        copy.start()
        sends.append(copy)
    flipped = jnp.transpose(sums_b[0:width, :])
    image = flipped[:RHS] + flipped[RHS:]

    left, _, _ = prepare_a(pack[...])
    high, low = strip(left, rows_b[...])
    out = product(vals_b[...], high)
    fine = product(eighth_b[...], low)
    image = image + (out[:RHS] + out[RHS:] + (fine[:RHS] + fine[RHS:2 * RHS]))

    for i in range(len(every)):
        copy = remote(send_a.at[i], back_a.at[i], ra_send.at[i], ra_recv.at[i], row_shift(1))
        copy.wait_recv()
        image = image + back_a[i]
    for o in range(1, nr):
        remote(send_b.at[o], back_b.at[o], rb_send.at[o], rb_recv.at[o], row_shift(1)).wait_recv()
        image = image + back_b[o]

    direction = dir_ref[...]
    residual = res_ref[...]
    image = GAIN * image + noise_level * direction

    lane = lax.broadcasted_iota(jnp.int32, (RHS, 128), 1)
    pairs = [dot_pair(residual, residual), dot_pair(direction, image), dot_pair(residual, image), dot_pair(image, image)]
    mixed = jnp.zeros((RHS, 128), F)
    for q, pair in enumerate(pairs):
        mixed = jnp.where(lane == q, pair[0], jnp.where(lane == q + 4, pair[1], mixed))
    value = jnp.sum(pltpu.roll(mixed, 0, 1, stride=8, stride_axis=0), axis=0, keepdims=True)
    first = lax.broadcasted_iota(jnp.int32, (1, 128), 1) % 8 < 4

    for size, buf, ssem, rsem, mine, peer in (
        (nr, red_row, rr_send, rr_recv, r, lambda e: (lax.rem(r + e, nr), c)),
        (nz * ny, red_col, rc_send, rc_recv, c, lambda e: (r, lax.rem(c + e, nz * ny))),
    ):
        buf[mine] = value
        for e in range(1, size):
            copy = remote(buf.at[mine], buf.at[mine], ssem.at[e], rsem.at[mine], peer(e))
            copy.start()
            sends.append(copy)
        for e in range(1, size):
            other = lax.rem(mine + e, size)
            remote(buf.at[other], buf.at[other], ssem.at[e], rsem.at[other], peer(e)).wait_recv()
        total, error = tree([(buf[e], jnp.zeros((1, 128), F)) for e in range(size)], add_pairs)
        value = jnp.where(first, total, total + pltpu.roll(error, 4, 1))

    place = lane - 8 * lax.broadcasted_iota(jnp.int32, (RHS, 128), 0)
    sums = [jnp.sum(jnp.where(place == q, value, 0.0), axis=1, keepdims=True) for q in range(8)]
    old, curve, cross, square = (settle((sums[q], sums[q + 4])) for q in range(4))
    step = old[0] / curve[0]
    change = scale_pair(square, -step)
    change = scale_pair(add_pairs((2.0 * cross[0], 2.0 * cross[1]), change), -step)
    new = settle(add_pairs(old, change))[0]
    fresh = residual - step * image
    out_ref[0:8] = sol_ref[...] + step * direction
    out_ref[8:16] = fresh
    out_ref[16:24] = fresh + new / old[0] * direction

    for copy in sends:
        copy.wait_send()

    def sent(i, carry):
        remote(send_a.at[i], back_a.at[i], ra_send.at[i], ra_recv.at[i], row_shift(1)).wait_send()
        return carry

    lax.fori_loop(0, len(every), sent, 0)


def solution(mesh):
    nr, nc = mesh.shape["row"], mesh.shape["col"]
    ny = 4 if nc == 32 else 2
    nz = nc // ny
    whole, half = offsets(nz, ny)
    na = len(whole) + len(half)

    def local(points, inv_length, solution_, residual, direction):
        width = points.shape[0]
        vmem = pl.BlockSpec(memory_space=pltpu.VMEM)
        dma = pltpu.SemaphoreType.DMA
        out = jax.ShapeDtypeStruct((3 * RHS, width), F)
        flat = pl.pallas_call(
            functools.partial(kernel, (nr, nz, ny, whole, half)),
            out_shape=out,
            in_specs=[pl.BlockSpec(memory_space=pltpu.HBM)] * 5,
            out_specs=vmem,
            scratch_shapes=[
                pltpu.VMEM((DIM, width), F),
                pltpu.VMEM((1, DIM), F),
                pltpu.VMEM((RHS, width), F),
                pltpu.VMEM((RHS, width), F),
                pltpu.VMEM((RHS, width), F),
                pltpu.VMEM((PACK, width), F),
                pltpu.VMEM((na, PACK, width), F),
                pltpu.VMEM((nr, PACK, width), F),
                pltpu.VMEM((nr * width, DEPTH), H),
                pltpu.VMEM((2 * RHS, nr * width), H),
                pltpu.VMEM((4 * RHS, nr * width), Q),
                pltpu.VMEM((nr * width, 2 * RHS), F),
                pltpu.VMEM((na, RHS, width), F),
                pltpu.VMEM((nr, RHS, width), F),
                pltpu.VMEM((na, RHS, width), F),
                pltpu.VMEM((nr, RHS, width), F),
                pltpu.VMEM((nr, 1, 128), F),
                pltpu.VMEM((nc, 1, 128), F),
                dma((5,)),
                dma((na,)), dma((na,)), dma((nr,)), dma((nr,)),
                dma((na,)), dma((na,)), dma((nr,)), dma((nr,)),
                dma((nr,)), dma((nr,)), dma((nc,)), dma((nc,)),
            ],
            compiler_params=pltpu.CompilerParams(
                collective_id=0, has_side_effects=True
            ),
            cost_estimate=pl.CostEstimate(flops=2 * 10**10, bytes_accessed=10**6, transcendentals=2 * 10**7),
        )(points.T, inv_length.reshape(1, DIM), solution_.T, residual.T, direction.T)
        return flat[0:8].T, flat[8:16].T, flat[16:24].T

    placed = (
        P(("row", "col"), None),
        P(),
        P(("row", "col"), None),
        P(("row", "col"), None),
        P(("row", "col"), None),
    )
    return jax.shard_map(
        local,
        mesh=mesh,
        in_specs=placed,
        out_specs=(P(("row", "col"), None),) * 3,
        check_vma=False,
    )
```

```python
import functools
import math

import jax
import jax.numpy as jnp
from jax import lax
from jax.experimental import pallas as pl
from jax.experimental.pallas import tpu as pltpu
from jax.sharding import PartitionSpec as P

F = jnp.float32
H = jnp.bfloat16
Q = jnp.float8_e4m3fn
MESH = pl.DeviceIdType.MESH
noise_level = 0.1
LOG2E = 1.0 / math.log(2.0)
SCALE = math.sqrt(5.0) * LOG2E
C1 = 3.0 * LOG2E
C0 = 3.0 * LOG2E * LOG2E
LIFT = 14.0
GAIN = 2.0 ** -LIFT / C0
DIM = 32
RHS = 8
PACK = DIM + RHS
NEAR = 2
DEPTH = 256


def offsets(nz, ny):
    def hop(d, n):
        return min(d, n - d)

    whole, half, load = [], [], {}
    every = sorted(
        ((dz, dy) for dz in range(nz) for dy in range(ny)),
        key=lambda o: (hop(o[0], nz) + hop(o[1], ny), o),
    )

    def charge(o):
        dz, dy = o
        out = {}
        if dz and 2 * dz != nz:
            out["z+" if 2 * dz < nz else "z-"] = hop(dz, nz)
        if dy and 2 * dy != ny:
            out["y+" if 2 * dy < ny else "y-"] = hop(dy, ny)
        return out

    for o in every:
        back = ((-o[0]) % nz, (-o[1]) % ny)
        if o == (0, 0):
            continue
        if o == back:
            half.append(o)
            continue
        if o in whole or back in whole:
            continue

        def cost(cand):
            trial = dict(load)
            for key, hops in charge(cand).items():
                trial[key] = trial.get(key, 0) + hops
            return sum(v * v for v in trial.values())

        pick = min((o, back), key=cost)
        for key, hops in charge(pick).items():
            load[key] = load.get(key, 0) + hops
        whole.append(pick)
    return whole, half


def pieces(x):
    first = x.astype(H).astype(F)
    rest = x - first
    second = rest.astype(H).astype(F)
    third = (rest - second).astype(H).astype(F)
    return first, second, third


def norms(scaled):
    return jnp.sum(scaled * scaled, axis=0, keepdims=True)


def stack_left(block, width):
    scaled = block[:DIM, :]
    h, m, l = pieces(scaled)
    qh, qm, ql = pieces(norms(scaled))
    one = jnp.ones((1, width), F)
    zero = jnp.zeros((DEPTH - 6 * DIM - 8, width), F)
    tail = jnp.concatenate([qh, qm, ql, one, one, one, zero[:2]], axis=0)
    return jnp.concatenate([h, h, m, m, h, l, tail, zero], axis=0)


def stack_right(block, width):
    scaled = block[:DIM, :]
    h, m, l = pieces(scaled)
    h, m, l = -2.0 * h, -2.0 * m, -2.0 * l
    qh, qm, ql = pieces(norms(scaled))
    one = jnp.ones((1, width), F)
    zero = jnp.zeros((DEPTH - 6 * DIM - 8, width), F)
    tail = jnp.concatenate([one, one, one, qh, qm, ql, zero[:2]], axis=0)
    return jnp.concatenate([h, m, h, m, l, h, tail, zero], axis=0)


def two_pieces(v):
    first = v.astype(H).astype(F)
    return jnp.concatenate([first, v - first], axis=0)


def two_eighths(v):
    first = v.astype(Q).astype(F)
    return jnp.concatenate([first, v - first, jnp.zeros_like(v), jnp.zeros_like(v)], axis=0)


def matern(x):
    x = jnp.maximum(x, 1e-30)
    t = x * lax.rsqrt(x)
    return (t * (t + C1) + C0) * jnp.exp2(LIFT - t)


def two_sum(a, b):
    s = a + b
    t = s - a
    return s, (a - (s - t)) + (b - t)


def split(a):
    c = a * 4097.0
    high = c - (c - a)
    return high, a - high


def two_product(a, b):
    p = a * b
    ah, al = split(a)
    bh, bl = split(b)
    return p, ((ah * bh - p) + ah * bl + al * bh) + al * bl


def add_pairs(a, b):
    s, e = two_sum(a[0], b[0])
    return s, e + (a[1] + b[1])


def settle(a):
    return two_sum(a[0], a[1])


def scale_pair(a, f):
    p, e = two_product(a[0], f)
    return settle((p, e + a[1] * f))


def tree(items, join):
    while len(items) > 1:
        items = [join(*items[i:i + 2]) if i + 1 < len(items) else items[i] for i in range(0, len(items), 2)]
    return items[0]


def dot_pair(a, b):
    p, e = two_product(a, b)
    n = a.shape[1] // 128
    pair = tree([(p[:, i * 128:(i + 1) * 128], e[:, i * 128:(i + 1) * 128]) for i in range(n)], add_pairs)
    for shift in (64, 32, 16, 8, 4, 2, 1):
        pair = add_pairs(pair, tuple(pltpu.roll(x, shift, 1) for x in pair))
    return pair


def kernel(
    plan,
    pts_hbm, inv_hbm, sol_hbm, res_hbm, dir_hbm,
    out_ref,
    pts_ref, inv_ref, sol_ref, res_ref, dir_ref,
    pack, gather_a, gather_b, rows_b, vals_b, eighth_b, sums_b,
    send_a, send_b, back_a, back_b, red_row, red_col,
    in_sem, ga_send, ga_recv, gb_send, gb_recv, ra_send, ra_recv, rb_send, rb_recv,
    rr_send, rr_recv, rc_send, rc_recv,
):
    nr, nz, ny, whole, half = plan
    nx = nr // 2
    width = pts_ref.shape[1]
    r = lax.axis_index("row")
    c = lax.axis_index("col")
    z, y = c // ny, c % ny
    x, core = r // 2, r % 2
    every = whole + half

    def shift(dz, dy):
        return (r, lax.rem(z + dz, nz) * ny + lax.rem(y + dy, ny))

    def row_shift(o, sign=1):
        dx = (o // 2) if sign > 0 else (nx - o // 2) % nx
        return (lax.rem(x + dx, nx) * 2 + lax.rem(core + o % 2, 2), c)

    def opposite(o):
        return ((nz - o[0]) % nz, (ny - o[1]) % ny)

    def remote(src, dst, send_sem, recv_sem, device):
        return pltpu.make_async_remote_copy(
            src_ref=src, dst_ref=dst, send_sem=send_sem, recv_sem=recv_sem,
            device_id=device, device_id_type=MESH,
        )

    barrier = pltpu.get_barrier_semaphore()
    for o in every:
        pl.semaphore_signal(barrier, inc=1, device_id=shift(*opposite(o)), device_id_type=MESH)
    for o in range(1, nr):
        pl.semaphore_signal(barrier, inc=1, device_id=row_shift(o), device_id_type=MESH)

    loads = [
        pltpu.make_async_copy(src, dst, in_sem.at[i])
        for i, (src, dst) in enumerate((
            (pts_hbm, pts_ref), (dir_hbm, dir_ref), (inv_hbm, inv_ref), (res_hbm, res_ref), (sol_hbm, sol_ref),
        ))
    ]
    for copy in loads:
        copy.start()
    for copy in loads[:3]:
        copy.wait()

    lengths = jnp.transpose(jnp.broadcast_to(inv_ref[...], (DIM, DIM)))[:, :1]
    pack[0:DIM, :] = pts_ref[...] * lengths * SCALE
    pack[DIM:PACK, :] = dir_ref[...]
    pl.semaphore_wait(barrier, len(every) + nr - 1)

    to_row = [
        remote(pack, gather_b.at[o], gb_send.at[o], gb_recv.at[o], row_shift(o, -1)) for o in range(1, nr)
    ]
    to_col = [
        remote(pack, gather_a.at[i], ga_send.at[i], ga_recv.at[i], shift(*o)) for i, o in enumerate(every)
    ]
    sends = to_row[:1] + to_col[:2] + to_row[1:] + to_col[2:]
    for copy in sends:
        copy.start()

    def prepare_b(o, block):
        at = pl.ds(pl.multiple_of(o * width, width), width)
        rows_b[at, :] = jnp.transpose(stack_right(block, width)).astype(H)
        vals_b[:, at] = two_pieces(block[DIM:PACK, :]).astype(H)
        eighth_b[:, at] = two_eighths(block[DIM:PACK, :]).astype(Q)

    sums_b[...] = jnp.zeros_like(sums_b)
    for copy in loads[3:]:
        copy.wait()
    prepare_b(0, pack[...])

    def arrive_b(o, carry):
        remote(pack, gather_b.at[o], gb_send.at[o], gb_recv.at[o], row_shift(1)).wait_recv()
        prepare_b(o, gather_b[o])
        return carry

    arrive_b(1, 0)

    def prepare_a(block):
        left = stack_left(block, width).astype(H)
        vals = jnp.transpose(two_pieces(block[DIM:PACK, :])).astype(H)
        eighth = jnp.transpose(two_eighths(block[DIM:PACK, :])[:2 * RHS]).astype(Q)
        return left, vals, eighth

    def strip(left, rows):
        k = matern(jnp.dot(rows, left, preferred_element_type=F))
        high = k.astype(H)
        low = (k - high.astype(F)).astype(Q)
        return high, low

    def product(a, b):
        return jnp.dot(a, b, preferred_element_type=F)

    def table(i, entries):
        out = jnp.int32(entries[0])
        for n in range(1, len(entries)):
            out = jnp.where(i == n, jnp.int32(entries[n]), out)
        return out

    def give_back(i, value, entries, base):
        send_a[i] = value
        back = [opposite(o) for o in entries]
        dz = table(i - base, [o[0] for o in back])
        dy = table(i - base, [o[1] for o in back])
        remote(send_a.at[i], back_a.at[i], ra_send.at[i], ra_recv.at[i], shift(dz, dy)).start()

    def work(i, at):
        left, vals, eighth = prepare_a(gather_a[i])
        high, low = strip(left, rows_b[at, :])
        sums_b[at, :] += product(high, vals)
        out = product(vals_b[:, at], high)
        sums_b[at, :] += product(low, eighth)
        fine = product(eighth_b[:, at], low)
        return out[:RHS] + out[RHS:] + (fine[:RHS] + fine[RHS:2 * RHS])

    def arrive_a(i):
        remote(pack, gather_a.at[i], ga_send.at[i], ga_recv.at[i], row_shift(1)).wait_recv()

    near = min(NEAR, len(whole))
    chip, rest = slice(0, 2 * width), slice(2 * width, nr * width)

    def near_strip(i, carry):
        arrive_a(i)
        send_a[i] = work(i, chip)
        return carry

    def whole_strip(i, carry):
        arrive_a(i)
        give_back(i, work(i, slice(None)), whole, 0)
        return carry

    def last_strip(i, carry):
        give_back(i, send_a[i] + work(i, rest), whole, 0)
        return carry

    lax.fori_loop(0, near, near_strip, 0)
    lax.fori_loop(2, nr, arrive_b, 0)
    lax.fori_loop(near, len(whole), whole_strip, 0)

    halves = []
    for dz, dy in half:
        halves.append(2 * z // nz if dz else 2 * y // ny)

    def half_strip(i, carry):
        n = i - len(whole)
        arrive_a(i)
        side = halves[0]
        for k in range(1, len(halves)):
            side = jnp.where(n == k, halves[k], side)
        at = pl.ds(pl.multiple_of((1 - side) * 2 * width, 2 * width), nr // 2 * width)
        give_back(i, work(i, at), half, len(whole))
        return carry

    lax.fori_loop(len(whole), len(every), half_strip, 0)
    lax.fori_loop(0, near, last_strip, 0)

    for o in range(1, nr):
        flipped = jnp.transpose(sums_b[o * width:(o + 1) * width, :])
        send_b[o] = flipped[:RHS] + flipped[RHS:]
        copy = remote(send_b.at[o], back_b.at[o], rb_send.at[o], rb_recv.at[o], row_shift(o))
        copy.start()
        sends.append(copy)
    flipped = jnp.transpose(sums_b[0:width, :])
    image = flipped[:RHS] + flipped[RHS:]

    left, _, _ = prepare_a(pack[...])
    high, low = strip(left, rows_b[...])
    out = product(vals_b[...], high)
    fine = product(eighth_b[...], low)
    image = image + (out[:RHS] + out[RHS:] + (fine[:RHS] + fine[RHS:2 * RHS]))

    direction = dir_ref[...]
    residual = res_ref[...]
    old_pair = dot_pair(residual, residual)

    for i in range(len(every)):
        copy = remote(send_a.at[i], back_a.at[i], ra_send.at[i], ra_recv.at[i], row_shift(1))
        copy.wait_recv()
        image = image + back_a[i]
    for o in range(1, nr):
        remote(send_b.at[o], back_b.at[o], rb_send.at[o], rb_recv.at[o], row_shift(1)).wait_recv()
        image = image + back_b[o]

    image = GAIN * image + noise_level * direction

    lane = lax.broadcasted_iota(jnp.int32, (RHS, 128), 1)
    pairs = [old_pair, dot_pair(direction, image), dot_pair(residual, image), dot_pair(image, image)]
    mixed = jnp.zeros((RHS, 128), F)
    for q, pair in enumerate(pairs):
        mixed = jnp.where(lane == q, pair[0], jnp.where(lane == q + 4, pair[1], mixed))
    value = jnp.sum(pltpu.roll(mixed, 0, 1, stride=8, stride_axis=0), axis=0, keepdims=True)
    first = lax.broadcasted_iota(jnp.int32, (1, 128), 1) % 8 < 4

    for size, buf, ssem, rsem, mine, peer in (
        (nr, red_row, rr_send, rr_recv, r, lambda e: (lax.rem(r + e, nr), c)),
        (nz * ny, red_col, rc_send, rc_recv, c, lambda e: (r, lax.rem(c + e, nz * ny))),
    ):
        buf[mine] = value
        for e in range(1, size):
            copy = remote(buf.at[mine], buf.at[mine], ssem.at[e], rsem.at[mine], peer(e))
            copy.start()
            sends.append(copy)
        for e in range(1, size):
            other = lax.rem(mine + e, size)
            remote(buf.at[other], buf.at[other], ssem.at[e], rsem.at[other], peer(e)).wait_recv()
        total, error = tree([(buf[e], jnp.zeros((1, 128), F)) for e in range(size)], add_pairs)
        value = jnp.where(first, total, total + pltpu.roll(error, 4, 1))

    place = lane - 8 * lax.broadcasted_iota(jnp.int32, (RHS, 128), 0)
    sums = [jnp.sum(jnp.where(place == q, value, 0.0), axis=1, keepdims=True) for q in range(8)]
    old, curve, cross, square = (settle((sums[q], sums[q + 4])) for q in range(4))
    step = old[0] / curve[0]
    change = scale_pair(square, -step)
    change = scale_pair(add_pairs((2.0 * cross[0], 2.0 * cross[1]), change), -step)
    new = settle(add_pairs(old, change))[0]
    fresh = residual - step * image
    out_ref[0:8] = sol_ref[...] + step * direction
    out_ref[8:16] = fresh
    out_ref[16:24] = fresh + new / old[0] * direction

    for copy in sends:
        copy.wait_send()

    def sent(i, carry):
        remote(send_a.at[i], back_a.at[i], ra_send.at[i], ra_recv.at[i], row_shift(1)).wait_send()
        return carry

    lax.fori_loop(0, len(every), sent, 0)


def solution(mesh):
    nr, nc = mesh.shape["row"], mesh.shape["col"]
    ny = 4 if nc == 32 else 2
    nz = nc // ny
    whole, half = offsets(nz, ny)
    na = len(whole) + len(half)

    def local(points, inv_length, solution_, residual, direction):
        width = points.shape[0]
        vmem = pl.BlockSpec(memory_space=pltpu.VMEM)
        dma = pltpu.SemaphoreType.DMA
        out = jax.ShapeDtypeStruct((3 * RHS, width), F)
        flat = pl.pallas_call(
            functools.partial(kernel, (nr, nz, ny, whole, half)),
            out_shape=out,
            in_specs=[pl.BlockSpec(memory_space=pltpu.HBM)] * 5,
            out_specs=vmem,
            scratch_shapes=[
                pltpu.VMEM((DIM, width), F),
                pltpu.VMEM((1, DIM), F),
                pltpu.VMEM((RHS, width), F),
                pltpu.VMEM((RHS, width), F),
                pltpu.VMEM((RHS, width), F),
                pltpu.VMEM((PACK, width), F),
                pltpu.VMEM((na, PACK, width), F),
                pltpu.VMEM((nr, PACK, width), F),
                pltpu.VMEM((nr * width, DEPTH), H),
                pltpu.VMEM((2 * RHS, nr * width), H),
                pltpu.VMEM((4 * RHS, nr * width), Q),
                pltpu.VMEM((nr * width, 2 * RHS), F),
                pltpu.VMEM((na, RHS, width), F),
                pltpu.VMEM((nr, RHS, width), F),
                pltpu.VMEM((na, RHS, width), F),
                pltpu.VMEM((nr, RHS, width), F),
                pltpu.VMEM((nr, 1, 128), F),
                pltpu.VMEM((nc, 1, 128), F),
                dma((5,)),
                dma((na,)), dma((na,)), dma((nr,)), dma((nr,)),
                dma((na,)), dma((na,)), dma((nr,)), dma((nr,)),
                dma((nr,)), dma((nr,)), dma((nc,)), dma((nc,)),
            ],
            compiler_params=pltpu.CompilerParams(
                collective_id=0, has_side_effects=True
            ),
            cost_estimate=pl.CostEstimate(flops=2 * 10**10, bytes_accessed=10**6, transcendentals=2 * 10**7),
        )(points.T, inv_length.reshape(1, DIM), solution_.T, residual.T, direction.T)
        return flat[0:8].T, flat[8:16].T, flat[16:24].T

    placed = (
        P(("row", "col"), None),
        P(),
        P(("row", "col"), None),
        P(("row", "col"), None),
        P(("row", "col"), None),
    )
    return jax.shard_map(
        local,
        mesh=mesh,
        in_specs=placed,
        out_specs=(P(("row", "col"), None),) * 3,
        check_vma=False,
    )
```
